128 devices in a mesh: wide: 16 (over y_lo, z, core), narrow: 8 (over y_hi, x).
Axes of the slice: x: 4, y: 4 (y_hi: 2, y_lo: 2; y = y_hi * 2 + y_lo), z: 4, core: 2. Of those that a mesh axis runs over, the one named last changes fastest.
Arguments:
- vit_tokens: bfloat16 [1024, 6144], P('wide', 'narrow'), may hold values from -18 to 18
- ln_gain: float32 [6144], P('narrow'), may hold values from 0.25 to 1.75
- w_fc1: bfloat16 [6144, 12288], P('narrow', 'wide'), may hold values from -0.078125 to 0.078125
- b_fc1: float32 [12288], P('wide'), may hold values from -3 to 3
- w_fc2: bfloat16 [12288, 6144], P('wide', 'narrow'), may hold values from -0.0546875 to 0.0546875
- b_fc2: float32 [6144], P('narrow'), may hold values from -3 to 3
- w_proj: bfloat16 [6144, 4096], P('narrow', 'wide'), may hold values from -0.078125 to 0.078125
- b_proj: float32 [4096], replicated, may hold values from -3 to 3
- text_states: bfloat16 [7168, 4096], P(('wide', 'narrow')), may hold values from -10 to 10
- rms_gain: float32 [4096], replicated, may hold values from 0.25 to 1.75
- w_gate: bfloat16 [4096, 8192], P('wide', 'narrow'), may hold values from -0.09375 to 0.09375
- w_up: bfloat16 [4096, 8192], P('wide', 'narrow'), may hold values from -0.09375 to 0.09375
- w_out: bfloat16 [8192, 4096], P('narrow', 'wide'), may hold values from -0.0625 to 0.0625
Outputs:
- vit_out: bfloat16 [1024, 6144], P('wide', 'narrow')
- ul2_image: bfloat16 [1024, 4096], P(('wide', 'narrow'))
- ul2_text: bfloat16 [7168, 4096], P(('wide', 'narrow'))
The draws below stay inside these ranges and needn't reach their ends.
All inputs are finite; a program needn't handle non-finite values.
Results may differ from the reference program's by a relative error of at most 0.03.
Values may be sent and summed in bfloat16 or wider, within the bound.
A program may use at most 128 MiB of HBM per device.

```python
import jax
import jax.numpy as jnp
from jax import lax

DV = 6144
FV = 12288
DU = 4096
FFU = 8192
TV = 1024
TT = 7168


def field_scales(key, rows, cols, rise):
    row_key, col_key = jax.random.split(key)
    row_scale = jnp.exp(jax.random.uniform(row_key, (rows, 1), jnp.float32, -1.15, 1.15))
    col_scale = jnp.exp(jax.random.uniform(col_key, (1, cols), jnp.float32, -1.15, 1.15))
    position = jnp.arange(cols, dtype=jnp.float32)[None, :] / cols
    return 0.25 * row_scale * col_scale * jnp.exp(rise * (position - 0.5))


def draw_vit_tokens(key, part):
    key = jax.random.fold_in(key, 11)
    base_key, scale_key = jax.random.split(key)
    values = jax.random.truncated_normal(base_key, -4.0, 4.0, (TV, DV), jnp.float32)
    return (values * field_scales(scale_key, TV, DV, 1.1)).astype(jnp.bfloat16)


def draw_text_states(key, part):
    key = jax.random.fold_in(key, 12)
    base_key, scale_key = jax.random.split(key)
    values = jax.random.truncated_normal(base_key, -4.0, 4.0, (TT, DU), jnp.float32)
    return (values * field_scales(scale_key, TT, DU, 0.0)).astype(jnp.bfloat16)


def shard_levels(own_key, dims, pieces, low, largest):
    factor_of, own = 1.0, jax.random.fold_in(own_key, 6)
    for dim, blocks in pieces:
        steps = jnp.exp(jax.random.uniform(jax.random.fold_in(own, dim), (blocks,), jnp.float32, low / len(pieces), largest / len(pieces)))
        factor_of = factor_of * jnp.repeat(steps, dims[dim] // blocks).reshape([-1 if axis == dim else 1 for axis in range(len(dims))])
    return factor_of


def centred(key, shape, scale, reach, shards=(), held_as=jnp.bfloat16):
    loudness = shard_levels(key, shape, shards, -0.22, 0.18) if shards else 1.0
    result = jax.random.normal(key, shape, jnp.float32) * scale * loudness
    return jnp.minimum(jnp.maximum(result, -reach), reach).astype(held_as)


def setup_inputs(seed: int = 0) -> dict:
    keys = jax.random.split(jax.random.key(seed), 14)
    vit_tokens = draw_vit_tokens(jax.random.fold_in(keys[13], 71), 0)
    ln_gain = jnp.clip(1.0 + 0.15 * jax.random.normal(keys[1], (DV,), jnp.float32), 0.25, 1.75)
    w_fc1 = centred(keys[2], (DV, FV), DV ** -0.5, 0.078125, ((0, 8), (1, 16)))
    b_fc1 = centred(keys[3], (FV,), 0.5, 3.0, ((0, 16),), jnp.float32)
    w_fc2 = centred(keys[4], (FV, DV), FV ** -0.5, 0.0546875, ((0, 16), (1, 8)))
    b_fc2 = centred(keys[5], (DV,), 0.5, 3.0, ((0, 8),), jnp.float32)
    w_proj = centred(keys[6], (DV, DU), DV ** -0.5, 0.078125, ((0, 8), (1, 16)))
    b_proj = centred(keys[7], (DU,), 0.5, 3.0, (), jnp.float32)
    text_states = draw_text_states(jax.random.fold_in(keys[13], 71), 0)
    rms_gain = jnp.clip(1.0 + 0.15 * jax.random.normal(keys[9], (DU,), jnp.float32), 0.25, 1.75)
    w_gate = centred(keys[10], (DU, FFU), DU ** -0.5, 0.09375, ((0, 16), (1, 8)))
    w_up = centred(keys[11], (DU, FFU), DU ** -0.5, 0.09375, ((0, 16), (1, 8)))
    w_out = centred(keys[12], (FFU, DU), FFU ** -0.5, 0.0625, ((0, 8), (1, 16)))
    return dict(vit_tokens=vit_tokens, ln_gain=ln_gain, w_fc1=w_fc1, b_fc1=b_fc1, w_fc2=w_fc2, b_fc2=b_fc2, w_proj=w_proj, b_proj=b_proj, text_states=text_states, rms_gain=rms_gain, w_gate=w_gate, w_up=w_up, w_out=w_out)


def layer_norm(values, gain):
    mean = lax.optimization_barrier(jnp.sum(values, -1, keepdims=True)) / DV
    square = lax.optimization_barrier(jnp.sum(values * values, -1, keepdims=True)) / DV
    variance = square - mean * mean
    return (values - mean) * lax.rsqrt(variance + 1e-06) * gain

def feed_forward(states, rms_gain, w_gate, w_up, w_out):
    wide_states = states.astype(jnp.float32)
    scale = lax.rsqrt(lax.optimization_barrier(jnp.mean(wide_states * wide_states, -1, keepdims=True)) + 1e-06)
    normed = (wide_states * scale * rms_gain).astype(jnp.bfloat16)
    gate = jnp.dot(normed, w_gate, preferred_element_type=jnp.float32)
    up_part = jnp.dot(normed, w_up, preferred_element_type=jnp.float32)
    inner = (jax.nn.silu(gate) * up_part).astype(jnp.bfloat16)
    out_sum = jnp.dot(inner, w_out, preferred_element_type=jnp.float32)
    return (wide_states + out_sum).astype(jnp.bfloat16)

def reference(vit_tokens, ln_gain, w_fc1, b_fc1, w_fc2, b_fc2, w_proj, b_proj, text_states, rms_gain, w_gate, w_up, w_out):
    tokens = vit_tokens.astype(jnp.float32)
    ln_rows = layer_norm(tokens, ln_gain).astype(jnp.bfloat16)
    fc1_sum = jnp.dot(ln_rows, w_fc1, preferred_element_type=jnp.float32)
    hidden = jax.nn.gelu(fc1_sum + b_fc1, approximate=False).astype(jnp.bfloat16)
    fc2_sum = jnp.dot(hidden, w_fc2, preferred_element_type=jnp.float32)
    vit_out = (tokens + fc2_sum + b_fc2).astype(jnp.bfloat16)
    proj_sum = jnp.dot(vit_out, w_proj, preferred_element_type=jnp.float32)
    image_states = (proj_sum + b_proj).astype(jnp.bfloat16)
    ul2_image = feed_forward(image_states, rms_gain, w_gate, w_up, w_out)
    ul2_text = feed_forward(text_states, rms_gain, w_gate, w_up, w_out)
    return (vit_out, ul2_image, ul2_text)
```

```python
import jax
import jax.numpy as jnp
from jax import lax
from jax.experimental import pallas as pl
from jax.experimental.pallas import tpu as pltpu
from jax.sharding import PartitionSpec as P

DV = 6144
DU = 4096
F32 = jnp.float32
BF16 = jnp.bfloat16
MESH = pl.DeviceIdType.MESH
EARLY = 48
LATE = 16
REST = [(0, 1), (0, 3), (1, 0), (0, 2), (1, 1), (1, 3), (1, 2)]
PLACES = [(0, 0)] + REST
ORDER = [(0, 0), (0, 3), (0, 1), (1, 0), (0, 2), (1, 3), (1, 1), (1, 2)]
R03, R01, R10, R02L, R02U, R13, R11, R12L, R12U, RSIB = range(10)


def dot(a, b):
    return jnp.dot(a, b, preferred_element_type=F32)


class Gather:
    def __init__(self, own, slot, half, dev, sib, send_sem, recv_sem, sends, local_sem=None):
        self.own, self.slot, self.half, self.dev, self.sib = own, slot, half, dev, sib
        self.send_sem, self.recv_sem, self.sends, self.count = send_sem, recv_sem, sends, 0
        self.local_sem = local_sem

    def send(self, src, dst, to, sem):
        copy = pltpu.make_async_remote_copy(
            src_ref=src,
            dst_ref=dst,
            send_sem=self.send_sem.at[self.count],
            recv_sem=self.recv_sem.at[sem],
            device_id=to,
            device_id_type=MESH,
        )
        copy.start()
        self.count += 1
        self.sends.append(copy)

    def wait(self, ref, sem):
        pltpu.make_async_remote_copy(
            src_ref=ref,
            dst_ref=ref,
            send_sem=self.send_sem.at[0],
            recv_sem=self.recv_sem.at[sem],
            device_id=self.dev(0, 1),
            device_id_type=MESH,
        ).wait_recv()

    def share(self, place, src=None):
        if self.sib is not None:
            ref = self.slot(*place, 0)
            self.send(ref if src is None else src, ref, self.sib, RSIB + PLACES.index(place))

    def begin(self):
        mine = self.slot(0, 0, 0)
        self.send(self.own, mine, self.dev(1, 0), R10)
        self.send(self.own, mine, self.dev(0, 1), R03)
        self.send(self.own, mine, self.dev(0, 3), R01)
        self.share((0, 0), self.own)
        if self.local_sem is not None:
            pltpu.make_async_copy(self.own, mine, self.local_sem).start()

    def forward(self, place, low, sem):
        ref = self.half(self.slot(*place, 0), 0 if low else 1)
        self.send(ref, ref, self.dev(0, 1 if low else 3), sem)

    def event(self, e):
        slot, half = self.slot, self.half
        if e == 1:
            self.wait(slot(0, 3, 0), R03)
            self.forward((0, 3), True, R02L)
            self.share((0, 3))
        elif e == 2:
            self.wait(slot(0, 1, 0), R01)
            self.forward((0, 1), False, R02U)
            self.share((0, 1))
        elif e == 3:
            ref = slot(1, 0, 0)
            self.wait(ref, R10)
            self.send(ref, ref, self.dev(0, 1), R13)
            self.send(ref, ref, self.dev(0, 3), R11)
            self.share((1, 0))
        elif e == 4:
            self.wait(half(slot(0, 2, 0), 0), R02L)
            self.wait(half(slot(0, 2, 0), 1), R02U)
            self.share((0, 2))
        elif e == 5:
            self.wait(slot(1, 3, 0), R13)
            self.forward((1, 3), True, R12L)
            self.share((1, 3))
        elif e == 6:
            self.wait(slot(1, 1, 0), R11)
            self.forward((1, 1), False, R12U)
            self.share((1, 1))
        else:
            self.wait(half(slot(1, 2, 0), 0), R12L)
            self.wait(half(slot(1, 2, 0), 1), R12U)
            self.share((1, 2))

    def wait_sibling(self, place):
        self.wait(self.slot(*place, 1), RSIB + PLACES.index(place))

    def wait_local(self):
        pltpu.make_async_copy(self.own, self.slot(0, 0, 0), self.local_sem).wait()

    def wait_siblings(self):
        self.wait_local()
        for place in ORDER:
            self.wait_sibling(place)


def kernel(
    vit_ref, ln_gain_ref, wfc1_ref, b1_ref, wfc2_ref, b2_ref, wproj_ref, bproj_ref,
    text_ref, rms_gain_ref, wgate_ref, wup_ref, wout_ref,
    vout_ref, res_ref,
    wg, wu, wo, wp,
    stat, xg, part, rs1, hg, sib2, rs2, pp, rp,
    re, rl, gacc, inner, inner_l, oe, rx, ys, yr, ol, ro, img,
    wss, wrs, tss, trs, lsem, dss, drs,
):
    w, n = lax.axis_index("wide"), lax.axis_index("narrow")
    c, z, yl = lax.rem(w, 2), lax.rem(w // 2, 4), w // 8
    x, yh = lax.rem(n, 4), n // 4

    def chip(dy, dz):
        return lax.rem(yl + dy, 2) * 4 + lax.rem(z + dz, 4)

    def wide_dev(dy, dz):
        return (chip(dy, dz) * 2 + c, n)

    def near(dy, dx):
        return lax.rem(yh + dy, 2) * 4 + lax.rem(x + dx, 4)

    def narrow_dev(dy, dx):
        return (w, near(dy, dx))

    sib = (chip(0, 0) * 2 + 1 - c, n)

    barrier = pltpu.get_barrier_semaphore()
    peers = [sib] + [wide_dev(*p) for p in REST] + [narrow_dev(*p) for p in REST]
    for peer in peers:
        pl.semaphore_signal(barrier, inc=1, device_id=peer, device_id_type=MESH)
    pl.semaphore_wait(barrier, len(peers))

    sends = []
    used = [0]

    def back(place):
        return (place[0], (4 - place[1]) % 4)

    def index(place):
        return REST.index(place)

    def send(src, dst, to, sem, keep=True):
        copy = pltpu.make_async_remote_copy(
            src_ref=src, dst_ref=dst, send_sem=dss.at[used[0]], recv_sem=drs.at[sem],
            device_id=to, device_id_type=MESH,
        )
        used[0] += 1
        copy.start()
        if keep:
            sends.append(copy)
        return copy

    def wait(ref, sem):
        pltpu.make_async_remote_copy(
            src_ref=ref, dst_ref=ref, send_sem=dss.at[0], recv_sem=drs.at[sem],
            device_id=sib, device_id_type=MESH,
        ).wait_recv()

    STAT, X, XSIB, RS1, HID, COMB, RS2, PROJ, LATE_IN, LATE_OUT, RX, RY = 0, 7, 14, 22, 36, 50, 52, 59, 66, 73, 80, 104

    def rows_of(buf, rows):
        def slot(dy, dz, other):
            start = (chip(dy, dz) * 2 + (1 - c if other else c)) * rows
            return buf.at[pl.ds(pl.multiple_of(start, rows), rows)]
        return slot

    def halves(rows):
        return lambda ref, k: ref.at[pl.ds(k * rows // 2, rows // 2)]

    def gather(i, own, buf, rows):
        return Gather(own, rows_of(buf, rows), halves(rows), wide_dev, sib, wss.at[i], wrs.at[i], sends, lsem.at[i])

    gate_g = gather(0, wgate_ref, wg, 256)
    up_g = gather(1, wup_ref, wu, 256)
    out_g = gather(2, wout_ref, wo, 1024)
    proj_g = gather(3, wproj_ref, wp, 768)

    def text_slot(dy, dx, other):
        return re.at[near(dy, dx)]

    text_g = Gather(
        re.at[n], text_slot, lambda ref, k: ref.at[:, pl.ds(k * DU // 2, DU // 2)],
        narrow_dev, None, tss, trs, sends,
    )

    def stats():
        rows = vit_ref[...].astype(F32)
        total = jnp.sum(rows, -1, keepdims=True)
        square = jnp.sum(rows * rows, -1, keepdims=True)
        lane = lax.broadcasted_iota(jnp.int32, (64, 128), 1)
        both = jnp.where(lane == 0, total, jnp.where(lane == 1, square, 0.0))
        turned = jnp.transpose(jnp.concatenate([both, jnp.zeros_like(both)], 0))
        stat[n] = turned[0:8]
        for p in REST:
            send(stat.at[n], stat.at[n], narrow_dev(*p), STAT + index(back(p)))

    def text_rows():
        rows = text_ref[...].astype(F32)
        scale = lax.rsqrt(jnp.mean(rows * rows, -1, keepdims=True) + 1e-06)
        normed = rows * scale * rms_gain_ref[...]
        re[n] = normed[0:EARLY].astype(BF16)

    def layer_norm():
        for p in REST:
            wait(stat.at[near(*p)], STAT + index(p))
        total = stat[0]
        for k in range(1, 8):
            total = total + stat[k]
        turned = jnp.transpose(jnp.concatenate([total, jnp.zeros((120, 128), F32)], 0))
        mean = turned[0:64, 0:1] / DV
        variance = turned[0:64, 1:2] / DV - mean * mean
        scale = lax.rsqrt(variance + 1e-06)
        rows = vit_ref[...].astype(F32)
        xg[w] = ((rows - mean) * scale * ln_gain_ref[...]).astype(BF16)
        for p in REST:
            send(xg.at[w], xg.at[w], wide_dev(*p), X + index(back(p)))
        send(xg.at[w], xg.at[w], sib, XSIB)

    def x_arrivals(h):
        order = [p for p in REST if p[0] == h]
        for p in order:
            ref = xg.at[chip(*p) * 2 + c]
            wait(ref, X + index(p))
            send(ref, ref, sib, XSIB + 1 + index(p))
        for p in PLACES:
            if p[0] == h:
                wait(xg.at[chip(*p) * 2 + 1 - c], XSIB + PLACES.index(p))

    def half_start(h):
        return lax.rem(yl + h, 2) * 4

    rs1_sends = {0: [], 1: []}

    def fc1(h):
        def step(i, carry):
            first = half_start(h) + 2 * i
            rows = xg[pl.ds(first * 2, 4)].reshape(256, 768)
            out = dot(rows, wfc1_ref[...]).astype(BF16).reshape(2, 8, 16, 768)
            part[:, first] = out[0]
            part[:, first + 1] = out[1]
            return carry
        lax.fori_loop(0, 2, step, 0)
        chips = pl.ds(half_start(h), 4)
        for p in REST:
            rs1_sends[h].append(
                send(part.at[near(*p), chips], rs1.at[n, chips], narrow_dev(*p), RS1 + 7 * h + index(back(p)), False)
            )

    def gelu(h):
        chips = pl.ds(half_start(h), 4)
        total = part[n, chips].astype(F32)
        for p in REST:
            wait(rs1.at[near(*p), chips], RS1 + 7 * h + index(p))
            total = total + rs1[near(*p), chips].astype(F32)
        v = total.reshape(64, 768) + b1_ref[...]
        hidden = 0.5 * v * (1.0 + lax.erf(v * (0.5 ** 0.5)))
        hg[n, chips] = hidden.astype(BF16).reshape(4, 16, 768)
        for p in REST:
            send(hg.at[n, chips], hg.at[n, chips], narrow_dev(*p), HID + 7 * h + index(back(p)))

    def fc2(h):
        chips = pl.ds(half_start(h), 4)
        for p in REST:
            wait(hg.at[near(*p), chips], HID + 7 * h + index(p))
        for copy in rs1_sends[h]:
            copy.wait_send()

        def step(i, carry):
            two = pl.ds(half_start(h) + 2 * i, 2)
            rows = hg[:, two].reshape(256, 768)
            part[:, two] = dot(rows, wfc2_ref[...]).astype(BF16).reshape(8, 2, 16, 768)
            return carry
        lax.fori_loop(0, 2, step, 0)
        send(part.at[pl.ds(4 * (1 - c), 4), chips], sib2.at[:, chips], sib, COMB + h)

    def combine(h):
        chips = pl.ds(half_start(h), 4)
        wait(sib2.at[:, chips], COMB + h)
        mine = part[pl.ds(4 * c, 4), chips].astype(F32)
        sib2[:, chips] = (mine + sib2[:, chips].astype(F32)).astype(BF16)
        for p in REST:
            if p[0] == h:
                send(sib2.at[:, chip(*p)], rs2.at[chip(0, 0)], wide_dev(*p), RS2 + index(back(p)))

    def vit_out():
        total = sib2[:, chip(0, 0)].astype(F32)
        for p in REST:
            wait(rs2.at[chip(*p)], RS2 + index(p))
            total = total + rs2[chip(*p)].astype(F32)
        rows = vit_ref[...].astype(F32) + total.reshape(64, 768) + b2_ref[...]
        vout_ref[...] = rows.astype(BF16)

    def proj():
        proj_g.wait_siblings()

        def step(i, carry):
            rows = vout_ref[...]
            low = dot(rows, wp[pl.ds(pl.multiple_of(i * 768, 768), 768)]).reshape(8, 8, 256)
            high = dot(rows, wp[pl.ds(pl.multiple_of((i + 8) * 768, 768), 768)]).reshape(8, 8, 256)
            pp[:, :, pl.ds(pl.multiple_of(i * 256, 256), 256)] = jnp.concatenate([low, high], 1).astype(BF16)
            return carry
        lax.fori_loop(0, 8, step, 0)
        for p in REST:
            send(pp.at[near(*p)], rp.at[n], narrow_dev(*p), PROJ + index(back(p)))

    def image_rows():
        total = pp[n].astype(F32)
        for p in REST:
            wait(rp.at[near(*p)], PROJ + index(p))
            total = total + rp[near(*p)].astype(F32)
        rows = jnp.concatenate([total[0:8], total[8:16]], 1) + bproj_ref[...]
        image = rows.astype(BF16).astype(F32)
        late = jnp.concatenate([text_ref[...].astype(F32)[EARLY:56], image], 0)
        img[...] = late
        scale = lax.rsqrt(jnp.mean(late * late, -1, keepdims=True) + 1e-06)
        rl[n] = (late * scale * rms_gain_ref[...]).astype(BF16)
        for p in REST:
            send(rl.at[n], rl.at[n], narrow_dev(*p), LATE_IN + index(back(p)))

    def gate_text():
        gate_g.wait_siblings()

        def step(i, carry):
            cols = pl.ds(pl.multiple_of(i * 256, 256), 256)
            gacc[:, cols] = dot(re[...].reshape(8 * EARLY, DU), wg[:, cols])
            return carry
        lax.fori_loop(0, 4, step, 0)

    def up_text():
        up_g.wait_siblings()

        def step(i, carry):
            cols = pl.ds(pl.multiple_of(i * 256, 256), 256)
            up = dot(re[...].reshape(8 * EARLY, DU), wu[:, cols])
            gate = gacc[:, cols]
            inner[:, cols] = (gate / (1.0 + jnp.exp(-gate)) * up).astype(BF16)
            return carry
        lax.fori_loop(0, 4, step, 0)

    def late_inner():
        for p in REST:
            wait(rl.at[near(*p)], LATE_IN + index(p))

        def step(i, carry):
            cols = pl.ds(pl.multiple_of(i * 256, 256), 256)
            rows = rl[...].reshape(8 * LATE, DU)
            gate = dot(rows, wg[:, cols])
            up = dot(rows, wu[:, cols])
            inner_l[:, cols] = (gate / (1.0 + jnp.exp(-gate)) * up).astype(BF16)
            return carry
        lax.fori_loop(0, 4, step, 0)

    def chunk_cols(k):
        return pl.ds(pl.multiple_of(chip(*ORDER[k]) * 512, 512), 512)

    def out_chunk(k):
        place = ORDER[k]
        if k == 0:
            out_g.wait_local()
        out_g.wait_sibling(place)

        def step(i, carry):
            who = chip(*place) * 2 + i
            block = wo[pl.ds(pl.multiple_of(who * 1024, 1024), 1024)]
            cols = pl.ds(pl.multiple_of(who * 256, 256), 256)
            oe[:, :, :, cols] = dot(inner[...], block).astype(BF16).reshape(2, 4, EARLY, 256)
            return carry
        lax.fori_loop(0, 2, step, 0)
        cols = chunk_cols(k)
        for dx in (1, 3, 2):
            to = lax.rem(x + dx, 4)
            send(oe.at[:, to, :, cols], rx.at[3 - dx, :, :, cols], narrow_dev(0, dx), RX + 3 * k + 3 - dx)

    def sum_x(k):
        cols = chunk_cols(k)
        total = oe[1 - yh, x, :, cols].astype(F32)
        for s in range(3):
            wait(rx.at[s, :, :, cols], RX + 3 * k + s)
            total = total + rx[s, 1 - yh, :, cols].astype(F32)
        ys[:, cols] = total.astype(BF16)
        send(ys.at[:, cols], yr.at[:, cols], narrow_dev(1, 0), RY + k)

    def finish(k):
        cols = chunk_cols(k)
        wait(yr.at[:, cols], RY + k)
        total = oe[yh, x, :, cols].astype(F32) + yr[:, cols].astype(F32)
        for s in range(3):
            total = total + rx[s, yh, :, cols].astype(F32)
        res_ref[0:EARLY, cols] = (text_ref[:, cols].astype(F32)[0:EARLY] + total).astype(BF16)

    def late_out():
        def step(i, carry):
            block = wo[pl.ds(pl.multiple_of(i * 1024, 1024), 1024)]
            cols = pl.ds(pl.multiple_of(i * 256, 256), 256)
            ol[:, :, cols] = dot(inner_l[...], block).astype(BF16).reshape(8, LATE, 256)
            return carry
        lax.fori_loop(0, 16, step, 0)
        for p in REST:
            send(ol.at[near(*p)], ro.at[n], narrow_dev(*p), LATE_OUT + index(back(p)))

    def late_finish():
        total = ol[n].astype(F32)
        for p in REST:
            wait(ro.at[near(*p)], LATE_OUT + index(p))
            total = total + ro[near(*p)].astype(F32)
        res_ref[EARLY:64] = (img[...] + total).astype(BF16)

    def events(g, *which):
        for e in which:
            g.event(e)

    stats()
    text_rows()
    text_g.begin()
    layer_norm()
    gate_g.begin()
    for h in (0, 1):
        x_arrivals(h)
        fc1(h)
    events(text_g, 1, 2, 3)
    events(gate_g, 1, 2, 3)
    proj_g.begin()
    gelu(0)
    gelu(1)
    events(text_g, 4, 5, 6, 7)
    events(gate_g, 4, 5, 6, 7)
    up_g.begin()
    fc2(0)
    fc2(1)
    combine(0)
    combine(1)
    events(proj_g, 1, 2, 3)
    gate_text()
    events(proj_g, 4, 5, 6, 7)
    vit_out()
    out_g.begin()
    proj()
    events(up_g, 1, 2, 3)
    image_rows()
    events(up_g, 4, 5, 6, 7)
    up_text()
    events(out_g, 1, 2, 3)
    late_inner()
    for k in range(4):
        out_chunk(k)
    for e, k in ((4, 4), (5, 5), (6, 6)):
        sum_x(k - 4)
        out_g.event(e)
        out_chunk(k)
    sum_x(3)
    out_g.event(7)
    out_chunk(7)
    late_out()
    for k in range(4, 8):
        sum_x(k)
    for k in range(8):
        finish(k)
    late_finish()
    for copy in sends:
        copy.wait_send()


def on_device(vit, ln_gain, w_fc1, b_fc1, w_fc2, b_fc2, w_proj, b_proj, text, rms_gain, w_gate, w_up, w_out):
    vmem = pl.BlockSpec(memory_space=pltpu.VMEM)
    hbm = pl.BlockSpec(memory_space=pl.ANY)
    bf = lambda *shape: pltpu.VMEM(shape, BF16)
    f32 = lambda *shape: pltpu.VMEM(shape, F32)
    dma = pltpu.SemaphoreType.DMA
    vit_out, result = pl.pallas_call(
        kernel,
        out_shape=(jax.ShapeDtypeStruct((64, 768), BF16), jax.ShapeDtypeStruct((64, DU), BF16)),
        in_specs=[vmem] * 6 + [hbm] + [vmem] * 3 + [hbm] * 3,
        out_specs=(vmem, vmem),
        scratch_shapes=[
            bf(4096, 1024), bf(4096, 1024), bf(16 * 1024, 256), bf(16 * 768, 256),
            f32(8, 8, 128), bf(16, 64, 768), bf(8, 8, 16, 768), bf(8, 8, 16, 768), bf(8, 8, 16, 768),
            bf(4, 8, 16, 768), bf(8, 4, 16, 768), bf(8, 16, 2048), bf(8, 16, 2048),
            bf(8, EARLY, DU), bf(8, LATE, DU), f32(8 * EARLY, 1024), bf(8 * EARLY, 1024), bf(8 * LATE, 1024),
            bf(2, 4, EARLY, DU), bf(3, 2, EARLY, DU), bf(EARLY, DU), bf(EARLY, DU),
            bf(8, LATE, DU), bf(8, LATE, DU), f32(LATE, DU),
            dma((4, 24)), dma((4, 20)), dma((12,)), dma((12,)), dma((4,)), dma((128,)), dma((112,)),
        ],
        compiler_params=pltpu.CompilerParams(
            collective_id=0, has_side_effects=True, vmem_limit_bytes=63 * 2**20
        ),
        cost_estimate=pl.CostEstimate(flops=15_300_000_000, bytes_accessed=12_000_000, transcendentals=1_000_000),
    )(
        vit, ln_gain.reshape(1, -1), w_fc1, b_fc1.reshape(1, -1), w_fc2, b_fc2.reshape(1, -1), w_proj,
        b_proj.reshape(1, -1), text, rms_gain.reshape(1, -1), w_gate, w_up, w_out,
    )
    return vit_out, result[56:64], result[0:56]


def solution(mesh):
    return jax.shard_map(
        on_device,
        mesh=mesh,
        in_specs=(
            P("wide", "narrow"),
            P("narrow"),
            P("narrow", "wide"),
            P("wide"),
            P("wide", "narrow"),
            P("narrow"),
            P("narrow", "wide"),
            P(),
            P(("wide", "narrow"), None),
            P(),
            P("wide", "narrow"),
            P("wide", "narrow"),
            P("narrow", "wide"),
        ),
        out_specs=(P("wide", "narrow"), P(("wide", "narrow"), None), P(("wide", "narrow"), None)),
        check_vma=False,
    )
```

```python
import jax
import jax.numpy as jnp
from jax import lax
from jax.experimental import pallas as pl
from jax.experimental.pallas import tpu as pltpu
from jax.sharding import PartitionSpec as P

DV = 6144
DU = 4096
F32 = jnp.float32
BF16 = jnp.bfloat16
MESH = pl.DeviceIdType.MESH
EARLY = 48
LATE = 16
REST = [(0, 1), (0, 3), (1, 0), (0, 2), (1, 1), (1, 3), (1, 2)]
PLACES = [(0, 0)] + REST
ORDER = [(0, 0), (0, 3), (0, 1), (1, 0), (0, 2), (1, 3), (1, 1), (1, 2)]
R03, R01, R10, R02L, R02U, R13, R11, R12L, R12U, RSIB = range(10)


def dot(a, b):
    return jnp.dot(a, b, preferred_element_type=F32)


class Gather:
    def __init__(self, own, slot, half, dev, sib, send_sem, recv_sem, sends, local_sem=None):
        self.own, self.slot, self.half, self.dev, self.sib = own, slot, half, dev, sib
        self.send_sem, self.recv_sem, self.sends, self.count = send_sem, recv_sem, sends, 0
        self.local_sem = local_sem

    def send(self, src, dst, to, sem):
        copy = pltpu.make_async_remote_copy(
            src_ref=src,
            dst_ref=dst,
            send_sem=self.send_sem.at[self.count],
            recv_sem=self.recv_sem.at[sem],
            device_id=to,
            device_id_type=MESH,
        )
        copy.start()
        self.count += 1
        self.sends.append(copy)

    def wait(self, ref, sem):
        pltpu.make_async_remote_copy(
            src_ref=ref,
            dst_ref=ref,
            send_sem=self.send_sem.at[0],
            recv_sem=self.recv_sem.at[sem],
            device_id=self.dev(0, 1),
            device_id_type=MESH,
        ).wait_recv()

    def share(self, place, src=None):
        if self.sib is not None:
            ref = self.slot(*place, 0)
            self.send(ref if src is None else src, ref, self.sib, RSIB + PLACES.index(place))

    def begin(self):
        mine = self.slot(0, 0, 0)
        self.send(self.own, mine, self.dev(1, 0), R10)
        self.send(self.own, mine, self.dev(0, 1), R03)
        self.send(self.own, mine, self.dev(0, 3), R01)
        self.share((0, 0), self.own)
        if self.local_sem is not None:
            pltpu.make_async_copy(self.own, mine, self.local_sem).start()

    def forward(self, place, low, sem):
        ref = self.half(self.slot(*place, 0), 0 if low else 1)
        self.send(ref, ref, self.dev(0, 1 if low else 3), sem)

    def event(self, e):
        slot, half = self.slot, self.half
        if e == 1:
            self.wait(slot(0, 3, 0), R03)
            self.forward((0, 3), True, R02L)
            self.share((0, 3))
        elif e == 2:
            self.wait(slot(0, 1, 0), R01)
            self.forward((0, 1), False, R02U)
            self.share((0, 1))
        elif e == 3:
            ref = slot(1, 0, 0)
            self.wait(ref, R10)
            self.send(ref, ref, self.dev(0, 1), R13)
            self.send(ref, ref, self.dev(0, 3), R11)
            self.share((1, 0))
        elif e == 4:
            self.wait(half(slot(0, 2, 0), 0), R02L)
            self.wait(half(slot(0, 2, 0), 1), R02U)
            self.share((0, 2))
        elif e == 5:
            self.wait(slot(1, 3, 0), R13)
            self.forward((1, 3), True, R12L)
            self.share((1, 3))
        elif e == 6:
            self.wait(slot(1, 1, 0), R11)
            self.forward((1, 1), False, R12U)
            self.share((1, 1))
        else:
            self.wait(half(slot(1, 2, 0), 0), R12L)
            self.wait(half(slot(1, 2, 0), 1), R12U)
            self.share((1, 2))

    def wait_sibling(self, place):
        self.wait(self.slot(*place, 1), RSIB + PLACES.index(place))

    def wait_local(self):
        pltpu.make_async_copy(self.own, self.slot(0, 0, 0), self.local_sem).wait()

    def wait_siblings(self):
        self.wait_local()
        for place in ORDER:
            self.wait_sibling(place)


def kernel(
    vit_hbm, ln_gain_ref, wfc1_hbm, b1_ref, wfc2_hbm, b2_ref, wproj_ref, bproj_ref,
    text_hbm, rms_gain_ref, wgate_ref, wup_ref, wout_ref,
    vout_ref, res_ref,
    vit_ref, text_ref, wfc1_ref, wfc2_ref,
    wg, wu, wo, wp,
    stat, xg, part, rs1, hg, sib2, rs2, vg, pp, rp, pa, qa,
    re, rl, gacc, inner, inner_l, oe, rx, ys, yr, ol, ro, img,
    wss, wrs, tss, trs, lsem, dss, drs,
):
    loads = [
        pltpu.make_async_copy(src, dst, lsem.at[4 + k])
        for k, (src, dst) in enumerate(
            ((vit_hbm, vit_ref), (text_hbm, text_ref), (wfc1_hbm, wfc1_ref), (wfc2_hbm, wfc2_ref))
        )
    ]
    for load in loads:
        load.start()

    def row(ref):
        return ref[...].reshape(1, -1)

    w, n = lax.axis_index("wide"), lax.axis_index("narrow")
    c, z, yl = lax.rem(w, 2), lax.rem(w // 2, 4), w // 8
    x, yh = lax.rem(n, 4), n // 4

    def chip(dy, dz):
        return lax.rem(yl + dy, 2) * 4 + lax.rem(z + dz, 4)

    def wide_dev(dy, dz):
        return (chip(dy, dz) * 2 + c, n)

    def near(dy, dx):
        return lax.rem(yh + dy, 2) * 4 + lax.rem(x + dx, 4)

    def narrow_dev(dy, dx):
        return (w, near(dy, dx))

    sib = (chip(0, 0) * 2 + 1 - c, n)

    barrier = pltpu.get_barrier_semaphore()
    peers = [sib] + [wide_dev(*p) for p in REST] + [narrow_dev(*p) for p in REST]
    for peer in peers:
        pl.semaphore_signal(barrier, inc=1, device_id=peer, device_id_type=MESH)
    pl.semaphore_wait(barrier, len(peers))

    sends = []
    used = [0]

    def back(place):
        return (place[0], (4 - place[1]) % 4)

    def index(place):
        return REST.index(place)

    def send(src, dst, to, sem, keep=True):
        copy = pltpu.make_async_remote_copy(
            src_ref=src, dst_ref=dst, send_sem=dss.at[used[0]], recv_sem=drs.at[sem],
            device_id=to, device_id_type=MESH,
        )
        used[0] += 1
        copy.start()
        if keep:
            sends.append(copy)
        return copy

    def wait(ref, sem):
        pltpu.make_async_remote_copy(
            src_ref=ref, dst_ref=ref, send_sem=dss.at[0], recv_sem=drs.at[sem],
            device_id=sib, device_id_type=MESH,
        ).wait_recv()

    STAT, X, XSIB, RS1, HID, COMB, RS2, PROJ, LATE_IN, LATE_OUT, RX, RY, VG, PA, WP = (
        0, 7, 14, 22, 36, 50, 52, 59, 66, 73, 80, 104, 112, 115, 118
    )

    def rows_of(buf, rows):
        def slot(dy, dz, other):
            start = (chip(dy, dz) * 2 + (1 - c if other else c)) * rows
            return buf.at[pl.ds(pl.multiple_of(start, rows), rows)]
        return slot

    def halves(rows):
        return lambda ref, k: ref.at[pl.ds(k * rows // 2, rows // 2)]

    def gather(i, own, buf, rows):
        return Gather(own, rows_of(buf, rows), halves(rows), wide_dev, sib, wss.at[i], wrs.at[i], sends, lsem.at[i])

    gate_g = gather(0, wgate_ref, wg, 256)
    up_g = gather(1, wup_ref, wu, 256)
    out_g = gather(2, wout_ref, wo, 1024)

    def text_slot(dy, dx, other):
        return re.at[near(dy, dx)]

    text_g = Gather(
        re.at[n], text_slot, lambda ref, k: ref.at[:, pl.ds(k * DU // 2, DU // 2)],
        narrow_dev, None, tss, trs, sends,
    )

    def stats():
        loads[0].wait()
        rows = vit_ref[...].astype(F32)
        total = jnp.sum(rows, -1, keepdims=True)
        square = jnp.sum(rows * rows, -1, keepdims=True)
        lane = lax.broadcasted_iota(jnp.int32, (64, 128), 1)
        both = jnp.where(lane == 0, total, jnp.where(lane == 1, square, 0.0))
        turned = jnp.transpose(jnp.concatenate([both, jnp.zeros_like(both)], 0))
        stat[n] = turned[0:8]
        for p in REST:
            send(stat.at[n], stat.at[n], narrow_dev(*p), STAT + index(back(p)))

    def text_rows():
        loads[1].wait()
        rows = text_ref[...].astype(F32)
        scale = lax.rsqrt(jnp.mean(rows * rows, -1, keepdims=True) + 1e-06)
        normed = rows * scale * row(rms_gain_ref)
        re[n] = normed[0:EARLY].astype(BF16)

    def layer_norm():
        for p in REST:
            wait(stat.at[near(*p)], STAT + index(p))
        total = stat[0]
        for k in range(1, 8):
            total = total + stat[k]
        turned = jnp.transpose(jnp.concatenate([total, jnp.zeros((120, 128), F32)], 0))
        mean = turned[0:64, 0:1] / DV
        variance = turned[0:64, 1:2] / DV - mean * mean
        scale = lax.rsqrt(variance + 1e-06)
        rows = vit_ref[...].astype(F32)
        xg[w] = ((rows - mean) * scale * row(ln_gain_ref)).astype(BF16)
        for p in REST:
            send(xg.at[w], xg.at[w], wide_dev(*p), X + index(back(p)))
        send(xg.at[w], xg.at[w], sib, XSIB)

    def x_arrivals(h):
        order = [p for p in REST if p[0] == h]
        for p in order:
            ref = xg.at[chip(*p) * 2 + c]
            wait(ref, X + index(p))
            send(ref, ref, sib, XSIB + 1 + index(p))
        for p in PLACES:
            if p[0] == h:
                wait(xg.at[chip(*p) * 2 + 1 - c], XSIB + PLACES.index(p))

    def half_start(h):
        return lax.rem(yl + h, 2) * 4

    rs1_sends = {0: [], 1: []}

    def fc1(h):
        if h == 0:
            loads[2].wait()

        def step(i, carry):
            first = half_start(h) + 2 * i
            rows = xg[pl.ds(first * 2, 4)].reshape(256, 768)
            out = dot(rows, wfc1_ref[...]).astype(BF16).reshape(2, 8, 16, 768)
            part[:, first] = out[0]
            part[:, first + 1] = out[1]
            return carry
        lax.fori_loop(0, 2, step, 0)
        chips = pl.ds(half_start(h), 4)
        for p in REST:
            rs1_sends[h].append(
                send(part.at[near(*p), chips], rs1.at[n, chips], narrow_dev(*p), RS1 + 7 * h + index(back(p)), False)
            )

    def gelu(h):
        chips = pl.ds(half_start(h), 4)
        total = part[n, chips].astype(F32)
        for p in REST:
            wait(rs1.at[near(*p), chips], RS1 + 7 * h + index(p))
            total = total + rs1[near(*p), chips].astype(F32)
        v = total.reshape(64, 768) + row(b1_ref)
        hidden = 0.5 * v * (1.0 + lax.erf(v * (0.5 ** 0.5)))
        hg[n, chips] = hidden.astype(BF16).reshape(4, 16, 768)
        for p in REST:
            send(hg.at[n, chips], hg.at[n, chips], narrow_dev(*p), HID + 7 * h + index(back(p)))

    def fc2(h):
        if h == 0:
            loads[3].wait()
        chips = pl.ds(half_start(h), 4)
        for p in REST:
            wait(hg.at[near(*p), chips], HID + 7 * h + index(p))
        for copy in rs1_sends[h]:
            copy.wait_send()

        def step(i, carry):
            two = pl.ds(half_start(h) + 2 * i, 2)
            rows = hg[:, two].reshape(256, 768)
            part[:, two] = dot(rows, wfc2_ref[...]).astype(BF16).reshape(8, 2, 16, 768)
            return carry
        lax.fori_loop(0, 2, step, 0)
        send(part.at[pl.ds(4 * (1 - c), 4), chips], sib2.at[:, chips], sib, COMB + h)

    def combine(h):
        chips = pl.ds(half_start(h), 4)
        wait(sib2.at[:, chips], COMB + h)
        mine = part[pl.ds(4 * c, 4), chips].astype(F32)
        sib2[:, chips] = (mine + sib2[:, chips].astype(F32)).astype(BF16)
        for p in REST:
            if p[0] == h:
                send(sib2.at[:, chip(*p)], rs2.at[chip(0, 0)], wide_dev(*p), RS2 + index(back(p)))

    def vit_out():
        total = sib2[:, chip(0, 0)].astype(F32)
        for p in REST:
            wait(rs2.at[chip(*p)], RS2 + index(p))
            total = total + rs2[chip(*p)].astype(F32)
        rows = vit_ref[...].astype(F32) + total.reshape(64, 768) + row(b2_ref)
        image = rows.astype(BF16)
        vout_ref[...] = image
        vg[z] = image
        for dz in (1, 3, 2):
            send(vg.at[z], vg.at[z], wide_dev(0, dz), VG + 3 - dz)

    def weights_at(dy, core):
        start = (lax.rem(yl + dy, 2) * 2 + core) * 768
        return wp.at[pl.ds(pl.multiple_of(start, 768), 768)]

    proj_local = pltpu.make_async_copy(wproj_ref, weights_at(0, c), lsem.at[3])

    def proj_begin():
        mine = weights_at(0, c)
        send(wproj_ref, mine, wide_dev(1, 0), WP)
        send(wproj_ref, mine, sib, WP + 1)
        proj_local.start()

    def proj_share():
        ref = weights_at(1, c)
        wait(ref, WP)
        send(ref, ref, sib, WP + 2)

    def proj():
        proj_local.wait()
        wait(weights_at(0, 1 - c), WP + 1)
        wait(weights_at(1, 1 - c), WP + 2)
        for dz in (1, 3, 2):
            wait(vg.at[lax.rem(z + dz, 4)], VG + dz - 1)
        for i in range(2):
            rows = vg[...].reshape(256, 768)
            low = dot(rows, wp[i * 768:(i + 1) * 768]).reshape(4, 8, 8, 256)
            high = dot(rows, wp[(i + 2) * 768:(i + 3) * 768]).reshape(4, 8, 8, 256)
            for k in range(4):
                pp[:, k, :, i * 256:(i + 1) * 256] = jnp.concatenate([low[k], high[k]], 1).astype(BF16)
        for p in REST:
            send(pp.at[near(*p)], rp.at[n], narrow_dev(*p), PROJ + index(back(p)))

    def proj_sum():
        total = pp[n].astype(F32)
        for p in REST:
            wait(rp.at[near(*p)], PROJ + index(p))
            total = total + rp[near(*p)].astype(F32)
        pa[...] = total
        qa[z] = pa[z]
        for dz in (1, 3, 2):
            send(pa.at[lax.rem(z + dz, 4)], qa.at[z], wide_dev(0, dz), PA + 3 - dz)

    def image_rows():
        for dz in (1, 3, 2):
            wait(qa.at[lax.rem(z + dz, 4)], PA + dz - 1)
        sums = [qa[k, 0:8] for k in range(4)] + [qa[k, 8:16] for k in range(4)]
        rows = jnp.concatenate(sums, 1) + row(bproj_ref)
        image = rows.astype(BF16).astype(F32)
        late = jnp.concatenate([text_ref[...].astype(F32)[EARLY:56], image], 0)
        img[...] = late
        scale = lax.rsqrt(jnp.mean(late * late, -1, keepdims=True) + 1e-06)
        rl[n] = (late * scale * row(rms_gain_ref)).astype(BF16)
        for p in REST:
            send(rl.at[n], rl.at[n], narrow_dev(*p), LATE_IN + index(back(p)))

    def gate_text():
        gate_g.wait_siblings()

        def step(i, carry):
            cols = pl.ds(pl.multiple_of(i * 256, 256), 256)
            gacc[:, cols] = dot(re[...].reshape(8 * EARLY, DU), wg[:, cols])
            return carry
        lax.fori_loop(0, 4, step, 0)

    def up_text():
        up_g.wait_siblings()

        def step(i, carry):
            cols = pl.ds(pl.multiple_of(i * 256, 256), 256)
            up = dot(re[...].reshape(8 * EARLY, DU), wu[:, cols])
            gate = gacc[:, cols]
            inner[:, cols] = (gate / (1.0 + jnp.exp(-gate)) * up).astype(BF16)
            return carry
        lax.fori_loop(0, 4, step, 0)

    def late_inner():
        for p in REST:
            wait(rl.at[near(*p)], LATE_IN + index(p))

        def step(i, carry):
            cols = pl.ds(pl.multiple_of(i * 256, 256), 256)
            rows = rl[...].reshape(8 * LATE, DU)
            gate = dot(rows, wg[:, cols])
            up = dot(rows, wu[:, cols])
            inner_l[:, cols] = (gate / (1.0 + jnp.exp(-gate)) * up).astype(BF16)
            return carry
        lax.fori_loop(0, 4, step, 0)

    def chunk_cols(k):
        return pl.ds(pl.multiple_of(chip(*ORDER[k]) * 512, 512), 512)

    def out_chunk(k):
        place = ORDER[k]
        if k == 0:
            out_g.wait_local()
        out_g.wait_sibling(place)

        def step(i, carry):
            who = chip(*place) * 2 + i
            block = wo[pl.ds(pl.multiple_of(who * 1024, 1024), 1024)]
            cols = pl.ds(pl.multiple_of(who * 256, 256), 256)
            oe[:, :, :, cols] = dot(inner[...], block).astype(BF16).reshape(2, 4, EARLY, 256)
            return carry
        lax.fori_loop(0, 2, step, 0)
        cols = chunk_cols(k)
        for dx in (1, 3, 2):
            to = lax.rem(x + dx, 4)
            send(oe.at[:, to, :, cols], rx.at[3 - dx, :, :, cols], narrow_dev(0, dx), RX + 3 * k + 3 - dx)

    def sum_x(k):
        cols = chunk_cols(k)
        total = oe[1 - yh, x, :, cols].astype(F32)
        for s in range(3):
            wait(rx.at[s, :, :, cols], RX + 3 * k + s)
            total = total + rx[s, 1 - yh, :, cols].astype(F32)
        ys[:, cols] = total.astype(BF16)
        send(ys.at[:, cols], yr.at[:, cols], narrow_dev(1, 0), RY + k)

    def finish(k):
        cols = chunk_cols(k)
        wait(yr.at[:, cols], RY + k)
        total = oe[yh, x, :, cols].astype(F32) + yr[:, cols].astype(F32)
        for s in range(3):
            total = total + rx[s, yh, :, cols].astype(F32)
        res_ref[0:EARLY, cols] = (text_ref[:, cols].astype(F32)[0:EARLY] + total).astype(BF16)

    def late_out():
        def step(i, carry):
            block = wo[pl.ds(pl.multiple_of(i * 1024, 1024), 1024)]
            cols = pl.ds(pl.multiple_of(i * 256, 256), 256)
            ol[:, :, cols] = dot(inner_l[...], block).astype(BF16).reshape(8, LATE, 256)
            return carry
        lax.fori_loop(0, 16, step, 0)
        for p in REST:
            send(ol.at[near(*p)], ro.at[n], narrow_dev(*p), LATE_OUT + index(back(p)))

    def late_finish():
        total = ol[n].astype(F32)
        for p in REST:
            wait(ro.at[near(*p)], LATE_OUT + index(p))
            total = total + ro[near(*p)].astype(F32)
        res_ref[EARLY:64] = (img[...] + total).astype(BF16)

    def events(g, *which):
        for e in which:
            g.event(e)

    stats()
    text_rows()
    gate_g.begin()
    text_g.begin()
    gate_g.event(1)
    gate_g.event(2)
    up_g.begin()
    text_g.event(3)
    layer_norm()
    gate_g.event(3)
    x_arrivals(0)
    fc1(0)
    x_arrivals(1)
    up_g.event(2)
    fc1(1)
    up_g.event(3)
    gelu(0)
    gate_g.event(5)
    gelu(1)
    text_g.event(1)
    up_g.event(1)
    gate_g.event(4)
    gate_g.event(6)
    text_g.event(6)
    up_g.event(5)
    out_g.begin()
    fc2(0)
    up_g.event(6)
    gate_g.event(7)
    text_g.event(2)
    text_g.event(5)
    fc2(1)
    text_g.event(4)
    combine(1)
    combine(0)
    proj_begin()
    up_g.event(7)
    text_g.event(7)
    up_g.event(4)
    gate_text()
    up_text()
    vit_out()
    out_chunk(0)
    out_g.event(1)
    out_g.event(2)
    out_chunk(2)
    proj_share()
    proj()
    out_g.event(4)
    out_g.event(3)
    out_chunk(4)
    proj_sum()
    out_chunk(3)
    image_rows()
    out_g.event(5)
    out_g.event(6)
    out_g.event(7)
    out_chunk(5)
    out_chunk(6)
    sum_x(0)
    sum_x(3)
    out_chunk(7)
    late_inner()
    out_chunk(1)
    sum_x(4)
    sum_x(2)
    late_out()
    sum_x(5)
    finish(3)
    sum_x(6)
    sum_x(7)
    sum_x(1)
    finish(7)
    finish(6)
    finish(4)
    finish(0)
    finish(2)
    finish(5)
    late_finish()
    finish(1)
    for copy in sends:
        copy.wait_send()


def split(vit_ref, rows_ref, vit_out_ref, image_ref, text_ref):
    vit_out_ref[...] = vit_ref[...]
    rows = rows_ref[...].astype(F32)
    image_ref[...] = rows[56:64].astype(BF16)
    text_ref[...] = rows[0:56].astype(BF16)


def on_device(vit, ln_gain, w_fc1, b_fc1, w_fc2, b_fc2, w_proj, b_proj, text, rms_gain, w_gate, w_up, w_out):
    vmem = pl.BlockSpec(memory_space=pltpu.VMEM)
    hbm = pl.BlockSpec(memory_space=pl.ANY)
    bf = lambda *shape: pltpu.VMEM(shape, BF16)
    f32 = lambda *shape: pltpu.VMEM(shape, F32)
    dma = pltpu.SemaphoreType.DMA
    vit_rows, result = pl.pallas_call(
        kernel,
        out_shape=(jax.ShapeDtypeStruct((64, 768), BF16), jax.ShapeDtypeStruct((64, DU), BF16)),
        in_specs=[hbm, vmem, hbm, vmem, hbm, vmem, hbm, vmem, hbm, vmem, hbm, hbm, hbm],
        out_specs=(vmem, vmem),
        scratch_shapes=[
            bf(64, 768), bf(56, DU), bf(768, 768), bf(768, 768),
            bf(4096, 1024), bf(4096, 1024), bf(16 * 1024, 256), bf(4 * 768, 256),
            f32(8, 8, 128), bf(16, 64, 768), bf(8, 8, 16, 768), bf(8, 8, 16, 768), bf(8, 8, 16, 768),
            bf(4, 8, 16, 768), bf(8, 4, 16, 768), bf(4, 64, 768),
            bf(8, 4, 16, 512), bf(8, 4, 16, 512), f32(4, 16, 512), f32(4, 16, 512),
            bf(8, EARLY, DU), bf(8, LATE, DU), f32(8 * EARLY, 1024), bf(8 * EARLY, 1024), bf(8 * LATE, 1024),
            bf(2, 4, EARLY, DU), bf(3, 2, EARLY, DU), bf(EARLY, DU), bf(EARLY, DU),
            bf(8, LATE, DU), bf(8, LATE, DU), f32(LATE, DU),
            dma((3, 24)), dma((3, 20)), dma((12,)), dma((12,)), dma((8,)), dma((128,)), dma((124,)),
        ],
        compiler_params=pltpu.CompilerParams(
            collective_id=0, has_side_effects=True, vmem_limit_bytes=63 * 2**20
        ),
        cost_estimate=pl.CostEstimate(flops=15_300_000_000, bytes_accessed=12_000_000, transcendentals=1_000_000),
    )(vit, ln_gain, w_fc1, b_fc1, w_fc2, b_fc2, w_proj, b_proj, text, rms_gain, w_gate, w_up, w_out)
    return pl.pallas_call(
        split,
        out_shape=(
            jax.ShapeDtypeStruct((64, 768), BF16),
            jax.ShapeDtypeStruct((8, DU), BF16),
            jax.ShapeDtypeStruct((56, DU), BF16),
        ),
        in_specs=[vmem] * 2,
        out_specs=(vmem, vmem, vmem),
    )(vit_rows, result)


def solution(mesh):
    return jax.shard_map(
        on_device,
        mesh=mesh,
        in_specs=(
            P("wide", "narrow"),
            P("narrow"),
            P("narrow", "wide"),
            P("wide"),
            P("wide", "narrow"),
            P("narrow"),
            P("narrow", "wide"),
            P(),
            P(("wide", "narrow"), None),
            P(),
            P("wide", "narrow"),
            P("wide", "narrow"),
            P("narrow", "wide"),
        ),
        out_specs=(P("wide", "narrow"), P(("wide", "narrow"), None), P(("wide", "narrow"), None)),
        check_vma=False,
    )
```

```python
import jax
import jax.numpy as jnp
from jax import lax
from jax.experimental import pallas as pl
from jax.experimental.pallas import tpu as pltpu
from jax.sharding import PartitionSpec as P

DV = 6144
DU = 4096
F32 = jnp.float32
BF16 = jnp.bfloat16
MESH = pl.DeviceIdType.MESH
EARLY = 48
LATE = 16
PAIR_FIRST = (1, 2, 3, 4,)
REST = [(0, 1), (0, 3), (1, 0), (0, 2), (1, 1), (1, 3), (1, 2)]
PLACES = [(0, 0)] + REST
ORDER = [(0, 0), (0, 3), (0, 1), (1, 0), (0, 2), (1, 3), (1, 1), (1, 2)]
R03, R01, R10, R02L, R02U, R13, R11, R12L, R12U, RSIB = range(10)


def dot(a, b):
    return jnp.dot(a, b, preferred_element_type=F32)


class Gather:
    def __init__(self, own, slot, half, dev, sib, send_sem, recv_sem, sends, local_sem=None):
        self.own, self.slot, self.half, self.dev, self.sib = own, slot, half, dev, sib
        self.send_sem, self.recv_sem, self.sends, self.count = send_sem, recv_sem, sends, 0
        self.local_sem = local_sem

    def send(self, src, dst, to, sem):
        copy = pltpu.make_async_remote_copy(
            src_ref=src,
            dst_ref=dst,
            send_sem=self.send_sem.at[self.count],
            recv_sem=self.recv_sem.at[sem],
            device_id=to,
            device_id_type=MESH,
        )
        copy.start()
        self.count += 1
        self.sends.append(copy)

    def wait(self, ref, sem):
        pltpu.make_async_remote_copy(
            src_ref=ref,
            dst_ref=ref,
            send_sem=self.send_sem.at[0],
            recv_sem=self.recv_sem.at[sem],
            device_id=self.dev(0, 1),
            device_id_type=MESH,
        ).wait_recv()

    def share(self, place, src=None):
        if self.sib is not None:
            ref = self.slot(*place, 0)
            self.send(ref if src is None else src, ref, self.sib, RSIB + PLACES.index(place))

    def begin(self):
        mine = self.slot(0, 0, 0)
        self.send(self.own, mine, self.dev(1, 0), R10)
        self.send(self.own, mine, self.dev(0, 1), R03)
        self.send(self.own, mine, self.dev(0, 3), R01)
        self.share((0, 0), self.own)
        if self.local_sem is not None:
            pltpu.make_async_copy(self.own, mine, self.local_sem).start()

    def forward(self, place, low, sem):
        ref = self.half(self.slot(*place, 0), 0 if low else 1)
        self.send(ref, ref, self.dev(0, 1 if low else 3), sem)

    def event(self, e):
        slot, half = self.slot, self.half
        if e == 1:
            self.wait(slot(0, 3, 0), R03)
            self.forward((0, 3), True, R02L)
            self.share((0, 3))
        elif e == 2:
            self.wait(slot(0, 1, 0), R01)
            self.forward((0, 1), False, R02U)
            self.share((0, 1))
        elif e == 3:
            ref = slot(1, 0, 0)
            self.wait(ref, R10)
            self.send(ref, ref, self.dev(0, 1), R13)
            self.send(ref, ref, self.dev(0, 3), R11)
            self.share((1, 0))
        elif e == 4:
            self.wait(half(slot(0, 2, 0), 0), R02L)
            self.wait(half(slot(0, 2, 0), 1), R02U)
            self.share((0, 2))
        elif e == 5:
            self.wait(slot(1, 3, 0), R13)
            self.forward((1, 3), True, R12L)
            self.share((1, 3))
        elif e == 6:
            self.wait(slot(1, 1, 0), R11)
            self.forward((1, 1), False, R12U)
            self.share((1, 1))
        else:
            self.wait(half(slot(1, 2, 0), 0), R12L)
            self.wait(half(slot(1, 2, 0), 1), R12U)
            self.share((1, 2))

    def wait_sibling(self, place):
        self.wait(self.slot(*place, 1), RSIB + PLACES.index(place))

    def wait_local(self):
        pltpu.make_async_copy(self.own, self.slot(0, 0, 0), self.local_sem).wait()

    def wait_siblings(self):
        self.wait_local()
        for place in ORDER:
            self.wait_sibling(place)


def kernel(
    vit_hbm, ln_gain_ref, wfc1_hbm, b1_ref, wfc2_hbm, b2_ref, wproj_ref, bproj_ref,
    text_hbm, rms_gain_ref, wgate_ref, wup_ref, wout_ref,
    vout_ref, res_ref,
    vit_ref, text_ref, wfc1_ref, wfc2_ref,
    wg, wu, wo, wp,
    stat, xg, part, rs1, hg, sib2, rs2, vg, pp, rp, pa, qa,
    re, rl, gacc, inner, inner_l, oe, rx, ryb, ys, yr, ol, ro, img,
    wss, wrs, tss, trs, lsem, dss, drs,
):
    loads = [
        pltpu.make_async_copy(src, dst, lsem.at[4 + k])
        for k, (src, dst) in enumerate(
            ((vit_hbm, vit_ref), (text_hbm, text_ref), (wfc1_hbm, wfc1_ref), (wfc2_hbm, wfc2_ref))
        )
    ]
    for load in loads:
        load.start()

    def row(ref):
        return ref[...].reshape(1, -1)

    w, n = lax.axis_index("wide"), lax.axis_index("narrow")
    c, z, yl = lax.rem(w, 2), lax.rem(w // 2, 4), w // 8
    x, yh = lax.rem(n, 4), n // 4

    def chip(dy, dz):
        return lax.rem(yl + dy, 2) * 4 + lax.rem(z + dz, 4)

    def wide_dev(dy, dz):
        return (chip(dy, dz) * 2 + c, n)

    def near(dy, dx):
        return lax.rem(yh + dy, 2) * 4 + lax.rem(x + dx, 4)

    def narrow_dev(dy, dx):
        return (w, near(dy, dx))

    sib = (chip(0, 0) * 2 + 1 - c, n)

    barrier = pltpu.get_barrier_semaphore()
    peers = [sib] + [wide_dev(*p) for p in REST] + [narrow_dev(*p) for p in REST]
    for peer in peers:
        pl.semaphore_signal(barrier, inc=1, device_id=peer, device_id_type=MESH)
    pl.semaphore_wait(barrier, len(peers))

    sends = []
    used = [0]

    def back(place):
        return (place[0], (4 - place[1]) % 4)

    def index(place):
        return REST.index(place)

    def send(src, dst, to, sem, keep=True):
        copy = pltpu.make_async_remote_copy(
            src_ref=src, dst_ref=dst, send_sem=dss.at[used[0]], recv_sem=drs.at[sem],
            device_id=to, device_id_type=MESH,
        )
        used[0] += 1
        copy.start()
        if keep:
            sends.append(copy)
        return copy

    def wait(ref, sem):
        pltpu.make_async_remote_copy(
            src_ref=ref, dst_ref=ref, send_sem=dss.at[0], recv_sem=drs.at[sem],
            device_id=sib, device_id_type=MESH,
        ).wait_recv()

    STAT, X, XSIB, RS1, HID, COMB, RS2, PROJ, LATE_IN, LATE_OUT, RX, RY, VG, PA, WP, RXB = (
        0, 7, 14, 22, 36, 50, 52, 59, 66, 73, 80, 104, 112, 115, 118, 124
    )

    def rows_of(buf, rows):
        def slot(dy, dz, other):
            start = (chip(dy, dz) * 2 + (1 - c if other else c)) * rows
            return buf.at[pl.ds(pl.multiple_of(start, rows), rows)]
        return slot

    def halves(rows):
        return lambda ref, k: ref.at[pl.ds(k * rows // 2, rows // 2)]

    def gather(i, own, buf, rows):
        return Gather(own, rows_of(buf, rows), halves(rows), wide_dev, sib, wss.at[i], wrs.at[i], sends, lsem.at[i])

    gate_g = gather(0, wgate_ref, wg, 256)
    up_g = gather(1, wup_ref, wu, 256)
    out_g = gather(2, wout_ref, wo, 1024)

    def text_slot(dy, dx, other):
        return re.at[near(dy, dx)]

    text_g = Gather(
        re.at[n], text_slot, lambda ref, k: ref.at[:, pl.ds(k * DU // 2, DU // 2)],
        narrow_dev, None, tss, trs, sends,
    )

    def stats():
        loads[0].wait()
        rows = vit_ref[...].astype(F32)
        total = jnp.sum(rows, -1, keepdims=True)
        square = jnp.sum(rows * rows, -1, keepdims=True)
        lane = lax.broadcasted_iota(jnp.int32, (64, 128), 1)
        both = jnp.where(lane == 0, total, jnp.where(lane == 1, square, 0.0))
        turned = jnp.transpose(jnp.concatenate([both, jnp.zeros_like(both)], 0))
        stat[n] = turned[0:8]
        for p in REST:
            send(stat.at[n], stat.at[n], narrow_dev(*p), STAT + index(back(p)))

    def text_rows():
        loads[1].wait()
        rows = text_ref[...].astype(F32)
        scale = lax.rsqrt(jnp.mean(rows * rows, -1, keepdims=True) + 1e-06)
        normed = rows * scale * row(rms_gain_ref)
        re[n] = normed[0:EARLY].astype(BF16)

    def layer_norm():
        for p in REST:
            wait(stat.at[near(*p)], STAT + index(p))
        total = stat[0]
        for k in range(1, 8):
            total = total + stat[k]
        turned = jnp.transpose(jnp.concatenate([total, jnp.zeros((120, 128), F32)], 0))
        mean = turned[0:64, 0:1] / DV
        variance = turned[0:64, 1:2] / DV - mean * mean
        scale = lax.rsqrt(variance + 1e-06)
        rows = vit_ref[...].astype(F32)
        xg[w] = ((rows - mean) * scale * row(ln_gain_ref)).astype(BF16)
        for p in REST:
            send(xg.at[w], xg.at[w], wide_dev(*p), X + index(back(p)))
        send(xg.at[w], xg.at[w], sib, XSIB)

    def x_arrivals(h):
        order = [p for p in REST if p[0] == h]
        for p in order:
            ref = xg.at[chip(*p) * 2 + c]
            wait(ref, X + index(p))
            send(ref, ref, sib, XSIB + 1 + index(p))
        for p in PLACES:
            if p[0] == h:
                wait(xg.at[chip(*p) * 2 + 1 - c], XSIB + PLACES.index(p))

    def half_start(h):
        return lax.rem(yl + h, 2) * 4

    rs1_sends = {0: [], 1: []}

    def fc1(h):
        if h == 0:
            loads[2].wait()

        def step(i, carry):
            first = half_start(h) + 2 * i
            rows = xg[pl.ds(first * 2, 4)].reshape(256, 768)
            out = dot(rows, wfc1_ref[...]).astype(BF16).reshape(2, 8, 16, 768)
            part[:, first] = out[0]
            part[:, first + 1] = out[1]
            return carry
        lax.fori_loop(0, 2, step, 0)
        chips = pl.ds(half_start(h), 4)
        for dy in (1, 0):
            for dx in (1, 3, 2):
                rs1_sends[h].append(
                    send(
                        part.at[near(dy, dx), chips], rs1.at[near(dy, 0), chips], narrow_dev(0, dx),
                        RS1 + 7 * h + index((dy, 4 - dx)), False,
                    )
                )

    def pair_sum(h):
        chips = pl.ds(half_start(h), 4)
        total = part[near(1, 0), chips].astype(F32)
        for dx in (1, 3, 2):
            wait(rs1.at[near(1, dx), chips], RS1 + 7 * h + index((1, dx)))
            total = total + rs1[near(1, dx), chips].astype(F32)
        part[near(1, 0), chips] = total.astype(BF16)
        rs1_sends[h].append(
            send(part.at[near(1, 0), chips], rs1.at[n, chips], narrow_dev(1, 0), RS1 + 7 * h + index((1, 0)), False)
        )

    def gelu(h):
        chips = pl.ds(half_start(h), 4)
        total = part[n, chips].astype(F32)
        for p in ((0, 1), (0, 3), (0, 2), (1, 0)):
            wait(rs1.at[near(*p), chips], RS1 + 7 * h + index(p))
            total = total + rs1[near(*p), chips].astype(F32)
        v = total.reshape(64, 768) + row(b1_ref)
        hidden = 0.5 * v * (1.0 + lax.erf(v * (0.5 ** 0.5)))
        hg[n, chips] = hidden.astype(BF16).reshape(4, 16, 768)
        for p in ((1, 0), (0, 1), (0, 3), (0, 2)):
            send(hg.at[n, chips], hg.at[n, chips], narrow_dev(*p), HID + 7 * h + index(back(p)))

    def pass_hidden(h):
        chips = pl.ds(half_start(h), 4)
        ref = hg.at[near(1, 0), chips]
        wait(ref, HID + 7 * h + index((1, 0)))
        for dx in (1, 3, 2):
            send(ref, ref, narrow_dev(0, dx), HID + 7 * h + index((1, 4 - dx)))

    def fc2(h):
        if h == 0:
            loads[3].wait()
        chips = pl.ds(half_start(h), 4)
        for p in [q for q in REST if q != (1, 0)]:
            wait(hg.at[near(*p), chips], HID + 7 * h + index(p))
        for copy in rs1_sends[h]:
            copy.wait_send()

        def step(i, carry):
            two = pl.ds(half_start(h) + 2 * i, 2)
            rows = hg[:, two].reshape(256, 768)
            part[:, two] = dot(rows, wfc2_ref[...]).astype(BF16).reshape(8, 2, 16, 768)
            return carry
        lax.fori_loop(0, 2, step, 0)
        send(part.at[pl.ds(4 * (1 - c), 4), chips], sib2.at[:, chips], sib, COMB + h)

    def combine(h):
        chips = pl.ds(half_start(h), 4)
        wait(sib2.at[:, chips], COMB + h)
        mine = part[pl.ds(4 * c, 4), chips].astype(F32)
        sib2[:, chips] = (mine + sib2[:, chips].astype(F32)).astype(BF16)
        for p in REST:
            if p[0] == h:
                send(sib2.at[:, chip(*p)], rs2.at[chip(0, 0)], wide_dev(*p), RS2 + index(back(p)))

    def vit_out():
        total = sib2[:, chip(0, 0)].astype(F32)
        for p in REST:
            wait(rs2.at[chip(*p)], RS2 + index(p))
            total = total + rs2[chip(*p)].astype(F32)
        rows = vit_ref[...].astype(F32) + total.reshape(64, 768) + row(b2_ref)
        image = rows.astype(BF16)
        vout_ref[...] = image
        vg[z] = image
        for dz in (1, 3, 2):
            send(vg.at[z], vg.at[z], wide_dev(0, dz), VG + 3 - dz)

    def weights_at(dy, core):
        start = (lax.rem(yl + dy, 2) * 2 + core) * 768
        return wp.at[pl.ds(pl.multiple_of(start, 768), 768)]

    proj_local = pltpu.make_async_copy(wproj_ref, weights_at(0, c), lsem.at[3])

    def proj_begin():
        mine = weights_at(0, c)
        send(wproj_ref, mine, wide_dev(1, 0), WP)
        send(wproj_ref, mine, sib, WP + 1)
        proj_local.start()

    def proj_share():
        ref = weights_at(1, c)
        wait(ref, WP)
        send(ref, ref, sib, WP + 2)

    def proj():
        proj_local.wait()
        wait(weights_at(0, 1 - c), WP + 1)
        wait(weights_at(1, 1 - c), WP + 2)
        for dz in (1, 3, 2):
            wait(vg.at[lax.rem(z + dz, 4)], VG + dz - 1)
        for i in range(2):
            rows = vg[...].reshape(256, 768)
            low = dot(rows, wp[i * 768:(i + 1) * 768]).reshape(4, 8, 8, 256)
            high = dot(rows, wp[(i + 2) * 768:(i + 3) * 768]).reshape(4, 8, 8, 256)
            for k in range(4):
                pp[:, k, :, i * 256:(i + 1) * 256] = jnp.concatenate([low[k], high[k]], 1).astype(BF16)
        for p in REST:
            send(pp.at[near(*p)], rp.at[n], narrow_dev(*p), PROJ + index(back(p)))

    def proj_sum():
        total = pp[n].astype(F32)
        for p in REST:
            wait(rp.at[near(*p)], PROJ + index(p))
            total = total + rp[near(*p)].astype(F32)
        pa[...] = total
        qa[z] = pa[z]
        for dz in (1, 3, 2):
            send(pa.at[lax.rem(z + dz, 4)], qa.at[z], wide_dev(0, dz), PA + 3 - dz)

    def image_rows():
        for dz in (1, 3, 2):
            wait(qa.at[lax.rem(z + dz, 4)], PA + dz - 1)
        sums = [qa[k, 0:8] for k in range(4)] + [qa[k, 8:16] for k in range(4)]
        rows = jnp.concatenate(sums, 1) + row(bproj_ref)
        image = rows.astype(BF16).astype(F32)
        late = jnp.concatenate([text_ref[...].astype(F32)[EARLY:56], image], 0)
        img[...] = late
        scale = lax.rsqrt(jnp.mean(late * late, -1, keepdims=True) + 1e-06)
        rl[n] = (late * scale * row(rms_gain_ref)).astype(BF16)
        for p in ((1, 0), (0, 1), (0, 3), (0, 2)):
            send(rl.at[n], rl.at[n], narrow_dev(*p), LATE_IN + index(back(p)))

    def pass_late():
        ref = rl.at[near(1, 0)]
        wait(ref, LATE_IN + index((1, 0)))
        for dx in (1, 3, 2):
            send(ref, ref, narrow_dev(0, dx), LATE_IN + index((1, 4 - dx)))

    def gate_text():
        gate_g.wait_siblings()

        def step(i, carry):
            cols = pl.ds(pl.multiple_of(i * 256, 256), 256)
            gacc[:, cols] = dot(re[...].reshape(8 * EARLY, DU), wg[:, cols])
            return carry
        lax.fori_loop(0, 4, step, 0)

    def up_text():
        up_g.wait_siblings()

        def step(i, carry):
            cols = pl.ds(pl.multiple_of(i * 256, 256), 256)
            up = dot(re[...].reshape(8 * EARLY, DU), wu[:, cols])
            gate = gacc[:, cols]
            inner[:, cols] = (gate / (1.0 + jnp.exp(-gate)) * up).astype(BF16)
            return carry
        lax.fori_loop(0, 4, step, 0)

    def late_inner():
        for p in [q for q in REST if q != (1, 0)]:
            wait(rl.at[near(*p)], LATE_IN + index(p))

        def step(i, carry):
            cols = pl.ds(pl.multiple_of(i * 256, 256), 256)
            rows = rl[...].reshape(8 * LATE, DU)
            gate = dot(rows, wg[:, cols])
            up = dot(rows, wu[:, cols])
            inner_l[:, cols] = (gate / (1.0 + jnp.exp(-gate)) * up).astype(BF16)
            return carry
        lax.fori_loop(0, 4, step, 0)

    def chunk_cols(k):
        return pl.ds(pl.multiple_of(chip(*ORDER[k]) * 512, 512), 512)

    def out_chunk(k):
        place = ORDER[k]
        if k == 0:
            out_g.wait_local()
        out_g.wait_sibling(place)

        def step(i, carry):
            who = chip(*place) * 2 + i
            block = wo[pl.ds(pl.multiple_of(who * 1024, 1024), 1024)]
            cols = pl.ds(pl.multiple_of(who * 256, 256), 256)
            oe[:, :, :, cols] = dot(inner[...], block).astype(BF16).reshape(2, 4, EARLY, 256)
            return carry
        lax.fori_loop(0, 2, step, 0)
        cols = chunk_cols(k)
        if k in PAIR_FIRST:
            send(oe.at[1 - yh, :, :, cols], ryb.at[:, :, cols], narrow_dev(1, 0), RX + 3 * k)
            return
        for dx in (1, 3, 2):
            to = lax.rem(x + dx, 4)
            send(oe.at[:, to, :, cols], rx.at[3 - dx, :, :, cols], narrow_dev(0, dx), RX + 3 * k + 3 - dx)

    def sum_x(k):
        cols = chunk_cols(k)
        if k in PAIR_FIRST:
            wait(ryb.at[:, :, cols], RX + 3 * k)
            total = oe[yh, :, :, cols].astype(F32) + ryb[:, :, cols].astype(F32)
            oe[yh, :, :, cols] = total.astype(BF16)
            for dx in (1, 3, 2):
                to = lax.rem(x + dx, 4)
                send(oe.at[yh, to, :, cols], rx.at[3 - dx, 0, :, cols], narrow_dev(0, dx), RXB + 3 * k + 3 - dx)
            return
        total = oe[1 - yh, x, :, cols].astype(F32)
        for s in range(3):
            wait(rx.at[s, :, :, cols], RX + 3 * k + s)
            total = total + rx[s, 1 - yh, :, cols].astype(F32)
        ys[:, cols] = total.astype(BF16)
        send(ys.at[:, cols], yr.at[:, cols], narrow_dev(1, 0), RY + k)

    def finish(k):
        cols = chunk_cols(k)
        total = oe[yh, x, :, cols].astype(F32)
        if k in PAIR_FIRST:
            for s in range(3):
                wait(rx.at[s, 0, :, cols], RXB + 3 * k + s)
                total = total + rx[s, 0, :, cols].astype(F32)
        else:
            wait(yr.at[:, cols], RY + k)
            total = total + yr[:, cols].astype(F32)
            for s in range(3):
                total = total + rx[s, yh, :, cols].astype(F32)
        res_ref[0:EARLY, cols] = (text_ref[:, cols].astype(F32)[0:EARLY] + total).astype(BF16)

    def late_out():
        def step(i, carry):
            block = wo[pl.ds(pl.multiple_of(i * 1024, 1024), 1024)]
            cols = pl.ds(pl.multiple_of(i * 256, 256), 256)
            ol[:, :, cols] = dot(inner_l[...], block).astype(BF16).reshape(8, LATE, 256)
            return carry
        lax.fori_loop(0, 16, step, 0)
        for p in REST:
            send(ol.at[near(*p)], ro.at[n], narrow_dev(*p), LATE_OUT + index(back(p)))

    def late_finish():
        total = ol[n].astype(F32)
        for p in REST:
            wait(ro.at[near(*p)], LATE_OUT + index(p))
            total = total + ro[near(*p)].astype(F32)
        res_ref[EARLY:64] = (img[...] + total).astype(BF16)

    def events(g, *which):
        for e in which:
            g.event(e)

    stats()
    gate_g.begin()
    layer_norm()
    up_g.begin()
    gate_g.event(3)
    x_arrivals(0)
    fc1(0)
    x_arrivals(1)
    fc1(1)
    pair_sum(0)
    pair_sum(1)
    up_g.event(3)
    up_g.event(2)
    gelu(0)
    gate_g.event(2)
    gelu(1)
    gate_g.event(1)
    text_rows()
    pass_hidden(0)
    pass_hidden(1)
    text_g.begin()
    proj_begin()
    fc2(0)
    combine(0)
    fc2(1)
    combine(1)
    up_g.event(1)
    gate_g.event(6)
    text_g.event(3)
    text_g.event(2)
    gate_g.event(4)
    gate_g.event(5)
    text_g.event(1)
    vit_out()
    text_g.event(4)
    proj_share()
    up_g.event(6)
    up_g.event(5)
    up_g.event(4)
    out_g.begin()
    text_g.event(5)
    text_g.event(6)
    text_g.event(7)
    proj()
    gate_g.event(7)
    gate_text()
    up_g.event(7)
    up_text()
    out_chunk(0)
    proj_sum()
    out_g.event(3)
    out_g.event(1)
    image_rows()
    out_g.event(2)
    out_chunk(2)
    out_chunk(3)
    pass_late()
    sum_x(2)
    out_g.event(6)
    out_g.event(5)
    out_chunk(1)
    out_chunk(6)
    sum_x(0)
    sum_x(3)
    out_chunk(5)
    out_g.event(4)
    late_inner()
    finish(2)
    out_g.event(7)
    out_chunk(4)
    sum_x(6)
    out_chunk(7)
    late_out()
    sum_x(1)
    sum_x(5)
    sum_x(7)
    sum_x(4)
    late_finish()
    finish(3)
    finish(5)
    finish(0)
    finish(6)
    finish(1)
    finish(7)
    finish(4)
    for copy in sends:
        copy.wait_send()


def split(vit_ref, rows_ref, vit_out_ref, image_ref, text_ref):
    vit_out_ref[...] = vit_ref[...]
    rows = rows_ref[...].astype(F32)
    image_ref[...] = rows[56:64].astype(BF16)
    text_ref[...] = rows[0:56].astype(BF16)


def on_device(vit, ln_gain, w_fc1, b_fc1, w_fc2, b_fc2, w_proj, b_proj, text, rms_gain, w_gate, w_up, w_out):
    vmem = pl.BlockSpec(memory_space=pltpu.VMEM)
    hbm = pl.BlockSpec(memory_space=pl.ANY)
    bf = lambda *shape: pltpu.VMEM(shape, BF16)
    f32 = lambda *shape: pltpu.VMEM(shape, F32)
    dma = pltpu.SemaphoreType.DMA
    vit_rows, result = pl.pallas_call(
        kernel,
        out_shape=(jax.ShapeDtypeStruct((64, 768), BF16), jax.ShapeDtypeStruct((64, DU), BF16)),
        in_specs=[hbm, vmem, hbm, vmem, hbm, vmem, hbm, vmem, hbm, vmem, hbm, hbm, hbm],
        out_specs=(vmem, vmem),
        scratch_shapes=[
            bf(64, 768), bf(56, DU), bf(768, 768), bf(768, 768),
            bf(4096, 1024), bf(4096, 1024), bf(16 * 1024, 256), bf(4 * 768, 256),
            f32(8, 8, 128), bf(16, 64, 768), bf(8, 8, 16, 768), bf(8, 8, 16, 768), bf(8, 8, 16, 768),
            bf(4, 8, 16, 768), bf(8, 4, 16, 768), bf(4, 64, 768),
            bf(8, 4, 16, 512), bf(8, 4, 16, 512), f32(4, 16, 512), f32(4, 16, 512),
            bf(8, EARLY, DU), bf(8, LATE, DU), f32(8 * EARLY, 1024), bf(8 * EARLY, 1024), bf(8 * LATE, 1024),
            bf(2, 4, EARLY, DU), bf(3, 2, EARLY, DU), bf(4, EARLY, DU), bf(EARLY, DU), bf(EARLY, DU),
            bf(8, LATE, DU), bf(8, LATE, DU), f32(LATE, DU),
            dma((3, 24)), dma((3, 20)), dma((12,)), dma((12,)), dma((8,)), dma((128,)), dma((148,)),
        ],
        compiler_params=pltpu.CompilerParams(
            collective_id=0, has_side_effects=True, vmem_limit_bytes=63 * 2**20
        ),
        cost_estimate=pl.CostEstimate(flops=15_300_000_000, bytes_accessed=12_000_000, transcendentals=1_000_000),
    )(vit, ln_gain, w_fc1, b_fc1, w_fc2, b_fc2, w_proj, b_proj, text, rms_gain, w_gate, w_up, w_out)
    return pl.pallas_call(
        split,
        out_shape=(
            jax.ShapeDtypeStruct((64, 768), BF16),
            jax.ShapeDtypeStruct((8, DU), BF16),
            jax.ShapeDtypeStruct((56, DU), BF16),
        ),
        in_specs=[vmem] * 2,
        out_specs=(vmem, vmem, vmem),
    )(vit_rows, result)


def solution(mesh):
    return jax.shard_map(
        on_device,
        mesh=mesh,
        in_specs=(
            P("wide", "narrow"),
            P("narrow"),
            P("narrow", "wide"),
            P("wide"),
            P("wide", "narrow"),
            P("narrow"),
            P("narrow", "wide"),
            P(),
            P(("wide", "narrow"), None),
            P(),
            P("wide", "narrow"),
            P("wide", "narrow"),
            P("narrow", "wide"),
        ),
        out_specs=(P("wide", "narrow"), P(("wide", "narrow"), None), P(("wide", "narrow"), None)),
        check_vma=False,
    )
```

```python
import jax
import jax.numpy as jnp
from jax import lax
from jax.experimental import pallas as pl
from jax.experimental.pallas import tpu as pltpu
from jax.sharding import PartitionSpec as P

DV = 6144
DU = 4096
F32 = jnp.float32
BF16 = jnp.bfloat16
MESH = pl.DeviceIdType.MESH
EARLY = 48
LATE = 16
PAIR_FIRST = (1, 2, 3, 4,)
REST = [(0, 1), (0, 3), (1, 0), (0, 2), (1, 1), (1, 3), (1, 2)]
PLACES = [(0, 0)] + REST
ORDER = [(0, 0), (0, 3), (0, 1), (1, 0), (0, 2), (1, 3), (1, 1), (1, 2)]
R03, R01, R10, R02L, R02U, R13, R11, R12L, R12U, RSIB = range(10)


def dot(a, b):
    return jnp.dot(a, b, preferred_element_type=F32)


class Gather:
    def __init__(self, own, slot, half, dev, sib, send_sem, recv_sem, sends, local_sem=None):
        self.own, self.slot, self.half, self.dev, self.sib = own, slot, half, dev, sib
        self.send_sem, self.recv_sem, self.sends, self.count = send_sem, recv_sem, sends, 0
        self.local_sem = local_sem

    def send(self, src, dst, to, sem):
        copy = pltpu.make_async_remote_copy(
            src_ref=src,
            dst_ref=dst,
            send_sem=self.send_sem.at[self.count],
            recv_sem=self.recv_sem.at[sem],
            device_id=to,
            device_id_type=MESH,
        )
        copy.start()
        self.count += 1
        self.sends.append(copy)

    def wait(self, ref, sem):
        pltpu.make_async_remote_copy(
            src_ref=ref,
            dst_ref=ref,
            send_sem=self.send_sem.at[0],
            recv_sem=self.recv_sem.at[sem],
            device_id=self.dev(0, 1),
            device_id_type=MESH,
        ).wait_recv()

    def share(self, place, src=None):
        if self.sib is not None:
            ref = self.slot(*place, 0)
            self.send(ref if src is None else src, ref, self.sib, RSIB + PLACES.index(place))

    def begin(self):
        mine = self.slot(0, 0, 0)
        self.send(self.own, mine, self.dev(1, 0), R10)
        self.send(self.own, mine, self.dev(0, 1), R03)
        self.send(self.own, mine, self.dev(0, 3), R01)
        self.share((0, 0), self.own)
        if self.local_sem is not None:
            pltpu.make_async_copy(self.own, mine, self.local_sem).start()

    def forward(self, place, low, sem):
        ref = self.half(self.slot(*place, 0), 0 if low else 1)
        self.send(ref, ref, self.dev(0, 1 if low else 3), sem)

    def event(self, e):
        slot, half = self.slot, self.half
        if e == 1:
            self.wait(slot(0, 3, 0), R03)
            self.forward((0, 3), True, R02L)
            self.share((0, 3))
        elif e == 2:
            self.wait(slot(0, 1, 0), R01)
            self.forward((0, 1), False, R02U)
            self.share((0, 1))
        elif e == 3:
            ref = slot(1, 0, 0)
            self.wait(ref, R10)
            self.send(ref, ref, self.dev(0, 1), R13)
            self.send(ref, ref, self.dev(0, 3), R11)
            self.share((1, 0))
        elif e == 4:
            self.wait(half(slot(0, 2, 0), 0), R02L)
            self.wait(half(slot(0, 2, 0), 1), R02U)
            self.share((0, 2))
        elif e == 5:
            self.wait(slot(1, 3, 0), R13)
            self.forward((1, 3), True, R12L)
            self.share((1, 3))
        elif e == 6:
            self.wait(slot(1, 1, 0), R11)
            self.forward((1, 1), False, R12U)
            self.share((1, 1))
        else:
            self.wait(half(slot(1, 2, 0), 0), R12L)
            self.wait(half(slot(1, 2, 0), 1), R12U)
            self.share((1, 2))

    def wait_sibling(self, place):
        self.wait(self.slot(*place, 1), RSIB + PLACES.index(place))

    def wait_local(self):
        pltpu.make_async_copy(self.own, self.slot(0, 0, 0), self.local_sem).wait()

    def wait_siblings(self):
        self.wait_local()
        for place in ORDER:
            self.wait_sibling(place)


def kernel(
    vit_hbm, ln_gain_ref, wfc1_hbm, b1_ref, wfc2_hbm, b2_ref, wproj_ref, bproj_ref,
    text_hbm, rms_gain_ref, wgate_ref, wup_ref, wout_ref,
    vout_ref, res_ref,
    vit_ref, text_ref, wfc1_ref, wfc2_ref,
    wg, wu, wo, wp,
    stat, xg, part, rs1, hg, sib2, rs2, vg, pp, rp, pa, qa,
    re, rl, gacc, inner, inner_l, oe, rx, ryb, ys, yr, ol, ro, img,
    wss, wrs, tss, trs, lsem, dss, drs,
):
    loads = [
        pltpu.make_async_copy(src, dst, lsem.at[4 + k])
        for k, (src, dst) in enumerate(
            ((vit_hbm, vit_ref), (text_hbm, text_ref), (wfc1_hbm, wfc1_ref), (wfc2_hbm, wfc2_ref))
        )
    ]
    for load in loads:
        load.start()

    def row(ref):
        return ref[...].reshape(1, -1)

    w, n = lax.axis_index("wide"), lax.axis_index("narrow")
    c, z, yl = lax.rem(w, 2), lax.rem(w // 2, 4), w // 8
    x, yh = lax.rem(n, 4), n // 4

    def chip(dy, dz):
        return lax.rem(yl + dy, 2) * 4 + lax.rem(z + dz, 4)

    def wide_dev(dy, dz):
        return (chip(dy, dz) * 2 + c, n)

    def near(dy, dx):
        return lax.rem(yh + dy, 2) * 4 + lax.rem(x + dx, 4)

    def narrow_dev(dy, dx):
        return (w, near(dy, dx))

    sib = (chip(0, 0) * 2 + 1 - c, n)

    barrier = pltpu.get_barrier_semaphore()
    peers = [sib] + [wide_dev(*p) for p in REST] + [narrow_dev(*p) for p in REST]
    for peer in peers:
        pl.semaphore_signal(barrier, inc=1, device_id=peer, device_id_type=MESH)
    pl.semaphore_wait(barrier, len(peers))

    sends = []
    used = [0]

    def back(place):
        return (place[0], (4 - place[1]) % 4)

    def index(place):
        return REST.index(place)

    def send(src, dst, to, sem, keep=True):
        copy = pltpu.make_async_remote_copy(
            src_ref=src, dst_ref=dst, send_sem=dss.at[used[0]], recv_sem=drs.at[sem],
            device_id=to, device_id_type=MESH,
        )
        used[0] += 1
        copy.start()
        if keep:
            sends.append(copy)
        return copy

    def wait(ref, sem):
        pltpu.make_async_remote_copy(
            src_ref=ref, dst_ref=ref, send_sem=dss.at[0], recv_sem=drs.at[sem],
            device_id=sib, device_id_type=MESH,
        ).wait_recv()

    STAT, X, XSIB, RS1, HID, COMB, RS2, PROJ, LATE_IN, LATE_OUT, RX, RY, VG, PA, WP, RXB, LATE_OUT2 = (
        0, 7, 14, 22, 36, 50, 52, 59, 66, 73, 80, 104, 112, 115, 118, 124, 148
    )

    def rows_of(buf, rows):
        def slot(dy, dz, other):
            start = (chip(dy, dz) * 2 + (1 - c if other else c)) * rows
            return buf.at[pl.ds(pl.multiple_of(start, rows), rows)]
        return slot

    def halves(rows):
        return lambda ref, k: ref.at[pl.ds(k * rows // 2, rows // 2)]

    def gather(i, own, buf, rows):
        return Gather(own, rows_of(buf, rows), halves(rows), wide_dev, sib, wss.at[i], wrs.at[i], sends, lsem.at[i])

    gate_g = gather(0, wgate_ref, wg, 256)
    up_g = gather(1, wup_ref, wu, 256)
    out_g = gather(2, wout_ref, wo, 1024)

    def text_slot(dy, dx, other):
        return re.at[near(dy, dx)]

    text_g = Gather(
        re.at[n], text_slot, lambda ref, k: ref.at[:, pl.ds(k * DU // 2, DU // 2)],
        narrow_dev, None, tss, trs, sends,
    )

    def stats():
        loads[0].wait()
        rows = vit_ref[...].astype(F32)
        total = jnp.sum(rows, -1, keepdims=True)
        square = jnp.sum(rows * rows, -1, keepdims=True)
        lane = lax.broadcasted_iota(jnp.int32, (64, 128), 1)
        both = jnp.where(lane == 0, total, jnp.where(lane == 1, square, 0.0))
        turned = jnp.transpose(jnp.concatenate([both, jnp.zeros_like(both)], 0))
        stat[n] = turned[0:8]
        for p in REST:
            send(stat.at[n], stat.at[n], narrow_dev(*p), STAT + index(back(p)))

    def text_rows():
        loads[1].wait()
        rows = text_ref[...].astype(F32)
        scale = lax.rsqrt(jnp.mean(rows * rows, -1, keepdims=True) + 1e-06)
        normed = rows * scale * row(rms_gain_ref)
        re[n] = normed[0:EARLY].astype(BF16)

    def layer_norm():
        for p in REST:
            wait(stat.at[near(*p)], STAT + index(p))
        total = stat[0]
        for k in range(1, 8):
            total = total + stat[k]
        turned = jnp.transpose(jnp.concatenate([total, jnp.zeros((120, 128), F32)], 0))
        mean = turned[0:64, 0:1] / DV
        variance = turned[0:64, 1:2] / DV - mean * mean
        scale = lax.rsqrt(variance + 1e-06)
        rows = vit_ref[...].astype(F32)
        xg[w] = ((rows - mean) * scale * row(ln_gain_ref)).astype(BF16)
        for p in REST:
            send(xg.at[w], xg.at[w], wide_dev(*p), X + index(back(p)))
        send(xg.at[w], xg.at[w], sib, XSIB)

    def x_arrivals(h):
        order = [p for p in REST if p[0] == h]
        for p in order:
            ref = xg.at[chip(*p) * 2 + c]
            wait(ref, X + index(p))
            send(ref, ref, sib, XSIB + 1 + index(p))
        for p in PLACES:
            if p[0] == h:
                wait(xg.at[chip(*p) * 2 + 1 - c], XSIB + PLACES.index(p))

    def half_start(h):
        return lax.rem(yl + h, 2) * 4

    rs1_sends = {0: [], 1: []}

    def fc1(h):
        if h == 0:
            loads[2].wait()

        def step(i, carry):
            first = half_start(h) + 2 * i
            rows = xg[pl.ds(first * 2, 4)].reshape(256, 768)
            out = dot(rows, wfc1_ref[...]).astype(BF16).reshape(2, 8, 16, 768)
            part[:, first] = out[0]
            part[:, first + 1] = out[1]
            return carry
        lax.fori_loop(0, 2, step, 0)
        chips = pl.ds(half_start(h), 4)
        for dy in (1, 0):
            for dx in (1, 3, 2):
                rs1_sends[h].append(
                    send(
                        part.at[near(dy, dx), chips], rs1.at[near(dy, 0), chips], narrow_dev(0, dx),
                        RS1 + 7 * h + index((dy, 4 - dx)), False,
                    )
                )

    def pair_sum(h):
        chips = pl.ds(half_start(h), 4)
        total = part[near(1, 0), chips].astype(F32)
        for dx in (1, 3, 2):
            wait(rs1.at[near(1, dx), chips], RS1 + 7 * h + index((1, dx)))
            total = total + rs1[near(1, dx), chips].astype(F32)
        part[near(1, 0), chips] = total.astype(BF16)
        rs1_sends[h].append(
            send(part.at[near(1, 0), chips], rs1.at[n, chips], narrow_dev(1, 0), RS1 + 7 * h + index((1, 0)), False)
        )

    def gelu(h):
        chips = pl.ds(half_start(h), 4)
        total = part[n, chips].astype(F32)
        for p in ((0, 1), (0, 3), (0, 2), (1, 0)):
            wait(rs1.at[near(*p), chips], RS1 + 7 * h + index(p))
            total = total + rs1[near(*p), chips].astype(F32)
        v = total.reshape(64, 768) + row(b1_ref)
        hidden = 0.5 * v * (1.0 + lax.erf(v * (0.5 ** 0.5)))
        hg[n, chips] = hidden.astype(BF16).reshape(4, 16, 768)
        for p in ((1, 0), (0, 1), (0, 3), (0, 2)):
            send(hg.at[n, chips], hg.at[n, chips], narrow_dev(*p), HID + 7 * h + index(back(p)))

    def pass_hidden(h):
        chips = pl.ds(half_start(h), 4)
        ref = hg.at[near(1, 0), chips]
        wait(ref, HID + 7 * h + index((1, 0)))
        for dx in (1, 3, 2):
            send(ref, ref, narrow_dev(0, dx), HID + 7 * h + index((1, 4 - dx)))

    def fc2(h):
        if h == 0:
            loads[3].wait()
        chips = pl.ds(half_start(h), 4)
        for p in [q for q in REST if q != (1, 0)]:
            wait(hg.at[near(*p), chips], HID + 7 * h + index(p))
        for copy in rs1_sends[h]:
            copy.wait_send()

        def step(i, carry):
            two = pl.ds(half_start(h) + 2 * i, 2)
            rows = hg[:, two].reshape(256, 768)
            part[:, two] = dot(rows, wfc2_ref[...]).astype(BF16).reshape(8, 2, 16, 768)
            return carry
        lax.fori_loop(0, 2, step, 0)
        send(part.at[pl.ds(4 * (1 - c), 4), chips], sib2.at[:, chips], sib, COMB + h)

    def combine(h):
        chips = pl.ds(half_start(h), 4)
        wait(sib2.at[:, chips], COMB + h)
        mine = part[pl.ds(4 * c, 4), chips].astype(F32)
        sib2[:, chips] = (mine + sib2[:, chips].astype(F32)).astype(BF16)
        for p in REST:
            if p[0] == h:
                send(sib2.at[:, chip(*p)], rs2.at[chip(0, 0)], wide_dev(*p), RS2 + index(back(p)))

    def vit_out():
        total = sib2[:, chip(0, 0)].astype(F32)
        for p in REST:
            wait(rs2.at[chip(*p)], RS2 + index(p))
            total = total + rs2[chip(*p)].astype(F32)
        rows = vit_ref[...].astype(F32) + total.reshape(64, 768) + row(b2_ref)
        image = rows.astype(BF16)
        vout_ref[...] = image
        vg[z] = image
        for dz in (1, 3, 2):
            send(vg.at[z], vg.at[z], wide_dev(0, dz), VG + 3 - dz)

    def weights_at(dy, core):
        start = (lax.rem(yl + dy, 2) * 2 + core) * 768
        return wp.at[pl.ds(pl.multiple_of(start, 768), 768)]

    proj_local = pltpu.make_async_copy(wproj_ref, weights_at(0, c), lsem.at[3])

    def proj_begin():
        mine = weights_at(0, c)
        send(wproj_ref, mine, wide_dev(1, 0), WP)
        send(wproj_ref, mine, sib, WP + 1)
        proj_local.start()

    def proj_share():
        ref = weights_at(1, c)
        wait(ref, WP)
        send(ref, ref, sib, WP + 2)

    def proj():
        proj_local.wait()
        wait(weights_at(0, 1 - c), WP + 1)
        wait(weights_at(1, 1 - c), WP + 2)
        for dz in (1, 3, 2):
            wait(vg.at[lax.rem(z + dz, 4)], VG + dz - 1)
        for i in range(2):
            rows = vg[...].reshape(256, 768)
            low = dot(rows, wp[i * 768:(i + 1) * 768]).reshape(4, 8, 8, 256)
            high = dot(rows, wp[(i + 2) * 768:(i + 3) * 768]).reshape(4, 8, 8, 256)
            for k in range(4):
                pp[:, k, :, i * 256:(i + 1) * 256] = jnp.concatenate([low[k], high[k]], 1).astype(BF16)
        for p in REST:
            send(pp.at[near(*p)], rp.at[n], narrow_dev(*p), PROJ + index(back(p)))

    def proj_sum():
        total = pp[n].astype(F32)
        for p in REST:
            wait(rp.at[near(*p)], PROJ + index(p))
            total = total + rp[near(*p)].astype(F32)
        pa[...] = total
        qa[z] = pa[z]
        for dz in (1, 3, 2):
            send(pa.at[lax.rem(z + dz, 4)], qa.at[z], wide_dev(0, dz), PA + 3 - dz)

    def image_rows():
        for dz in (1, 3, 2):
            wait(qa.at[lax.rem(z + dz, 4)], PA + dz - 1)
        sums = [qa[k, 0:8] for k in range(4)] + [qa[k, 8:16] for k in range(4)]
        rows = jnp.concatenate(sums, 1) + row(bproj_ref)
        image = rows.astype(BF16).astype(F32)
        late = jnp.concatenate([text_ref[...].astype(F32)[EARLY:56], image], 0)
        img[...] = late
        scale = lax.rsqrt(jnp.mean(late * late, -1, keepdims=True) + 1e-06)
        rl[n] = (late * scale * row(rms_gain_ref)).astype(BF16)
        for p in ((1, 0), (0, 1), (0, 3), (0, 2)):
            send(rl.at[n], rl.at[n], narrow_dev(*p), LATE_IN + index(back(p)))

    def pass_late():
        ref = rl.at[near(1, 0)]
        wait(ref, LATE_IN + index((1, 0)))
        for dx in (1, 3, 2):
            send(ref, ref, narrow_dev(0, dx), LATE_IN + index((1, 4 - dx)))

    def gate_text():
        gate_g.wait_siblings()

        def step(i, carry):
            cols = pl.ds(pl.multiple_of(i * 256, 256), 256)
            gacc[:, cols] = dot(re[...].reshape(8 * EARLY, DU), wg[:, cols])
            return carry
        lax.fori_loop(0, 4, step, 0)

    def up_text():
        up_g.wait_siblings()

        def step(i, carry):
            cols = pl.ds(pl.multiple_of(i * 256, 256), 256)
            up = dot(re[...].reshape(8 * EARLY, DU), wu[:, cols])
            gate = gacc[:, cols]
            inner[:, cols] = (gate / (1.0 + jnp.exp(-gate)) * up).astype(BF16)
            return carry
        lax.fori_loop(0, 4, step, 0)

    def late_inner():
        for p in [q for q in REST if q != (1, 0)]:
            wait(rl.at[near(*p)], LATE_IN + index(p))

        def step(i, carry):
            cols = pl.ds(pl.multiple_of(i * 256, 256), 256)
            rows = rl[...].reshape(8 * LATE, DU)
            gate = dot(rows, wg[:, cols])
            up = dot(rows, wu[:, cols])
            inner_l[:, cols] = (gate / (1.0 + jnp.exp(-gate)) * up).astype(BF16)
            return carry
        lax.fori_loop(0, 4, step, 0)

    def chunk_cols(k):
        return pl.ds(pl.multiple_of(chip(*ORDER[k]) * 512, 512), 512)

    def out_chunk(k):
        place = ORDER[k]
        if k == 0:
            out_g.wait_local()
        out_g.wait_sibling(place)

        def step(i, carry):
            who = chip(*place) * 2 + i
            block = wo[pl.ds(pl.multiple_of(who * 1024, 1024), 1024)]
            cols = pl.ds(pl.multiple_of(who * 256, 256), 256)
            oe[:, :, :, cols] = dot(inner[...], block).astype(BF16).reshape(2, 4, EARLY, 256)
            return carry
        lax.fori_loop(0, 2, step, 0)
        cols = chunk_cols(k)
        if k in PAIR_FIRST:
            send(oe.at[1 - yh, :, :, cols], ryb.at[:, :, cols], narrow_dev(1, 0), RX + 3 * k)
            return
        for dx in (1, 3, 2):
            to = lax.rem(x + dx, 4)
            send(oe.at[:, to, :, cols], rx.at[3 - dx, :, :, cols], narrow_dev(0, dx), RX + 3 * k + 3 - dx)

    def sum_x(k):
        cols = chunk_cols(k)
        if k in PAIR_FIRST:
            wait(ryb.at[:, :, cols], RX + 3 * k)
            total = oe[yh, :, :, cols].astype(F32) + ryb[:, :, cols].astype(F32)
            oe[yh, :, :, cols] = total.astype(BF16)
            for dx in (1, 3, 2):
                to = lax.rem(x + dx, 4)
                send(oe.at[yh, to, :, cols], rx.at[3 - dx, 0, :, cols], narrow_dev(0, dx), RXB + 3 * k + 3 - dx)
            return
        total = oe[1 - yh, x, :, cols].astype(F32)
        for s in range(3):
            wait(rx.at[s, :, :, cols], RX + 3 * k + s)
            total = total + rx[s, 1 - yh, :, cols].astype(F32)
        ys[:, cols] = total.astype(BF16)
        send(ys.at[:, cols], yr.at[:, cols], narrow_dev(1, 0), RY + k)

    def finish(k):
        cols = chunk_cols(k)
        total = oe[yh, x, :, cols].astype(F32)
        if k in PAIR_FIRST:
            for s in range(3):
                wait(rx.at[s, 0, :, cols], RXB + 3 * k + s)
                total = total + rx[s, 0, :, cols].astype(F32)
        else:
            wait(yr.at[:, cols], RY + k)
            total = total + yr[:, cols].astype(F32)
            for s in range(3):
                total = total + rx[s, yh, :, cols].astype(F32)
        res_ref[0:EARLY, cols] = (text_ref[:, cols].astype(F32)[0:EARLY] + total).astype(BF16)

    def late_half(e):
        return pl.ds(e * DU // 2, DU // 2)

    def late_out(e):
        def step(i, carry):
            block = wo[pl.ds(pl.multiple_of(i * 1024, 1024), 1024)]
            cols = pl.ds(pl.multiple_of(i * 256, 256), 256)
            ol[:, :, cols] = dot(inner_l[...], block).astype(BF16).reshape(8, LATE, 256)
            return carry
        lax.fori_loop(8 * e, 8 * e + 8, step, 0)
        for p in REST:
            send(
                ol.at[near(*p), :, late_half(e)], ro.at[n, :, late_half(e)], narrow_dev(*p),
                (LATE_OUT, LATE_OUT2)[e] + index(back(p)),
            )

    def late_finish():
        total = ol[n].astype(F32)
        for p in REST:
            for e in range(2):
                wait(ro.at[near(*p), :, late_half(e)], (LATE_OUT, LATE_OUT2)[e] + index(p))
            total = total + ro[near(*p)].astype(F32)
        res_ref[EARLY:64] = (img[...] + total).astype(BF16)

    def events(g, *which):
        for e in which:
            g.event(e)

    stats()
    gate_g.begin()
    layer_norm()
    up_g.begin()
    gate_g.event(3)
    x_arrivals(0)
    fc1(0)
    x_arrivals(1)
    fc1(1)
    pair_sum(0)
    pair_sum(1)
    up_g.event(3)
    up_g.event(2)
    gelu(0)
    gate_g.event(2)
    gelu(1)
    gate_g.event(1)
    text_rows()
    pass_hidden(0)
    pass_hidden(1)
    text_g.begin()
    proj_begin()
    fc2(0)
    combine(0)
    fc2(1)
    combine(1)
    up_g.event(1)
    gate_g.event(6)
    text_g.event(3)
    text_g.event(2)
    gate_g.event(4)
    gate_g.event(5)
    text_g.event(1)
    vit_out()
    text_g.event(4)
    proj_share()
    up_g.event(6)
    up_g.event(5)
    up_g.event(4)
    out_g.begin()
    text_g.event(5)
    text_g.event(6)
    text_g.event(7)
    proj()
    gate_g.event(7)
    gate_text()
    up_g.event(7)
    up_text()
    out_chunk(0)
    proj_sum()
    out_g.event(3)
    out_g.event(1)
    image_rows()
    out_g.event(2)
    out_chunk(2)
    out_chunk(3)
    pass_late()
    sum_x(2)
    out_g.event(6)
    out_g.event(5)
    out_chunk(1)
    out_chunk(6)
    sum_x(0)
    sum_x(3)
    out_chunk(5)
    out_g.event(4)
    late_inner()
    finish(2)
    out_g.event(7)
    out_chunk(4)
    sum_x(6)
    out_chunk(7)
    late_out(0)
    late_out(1)
    sum_x(1)
    sum_x(5)
    sum_x(7)
    sum_x(4)
    late_finish()
    finish(3)
    finish(5)
    finish(0)
    finish(6)
    finish(1)
    finish(7)
    finish(4)
    for copy in sends:
        copy.wait_send()


def split(vit_ref, rows_ref, vit_out_ref, image_ref, text_ref):
    vit_out_ref[...] = vit_ref[...]
    rows = rows_ref[...].astype(F32)
    image_ref[...] = rows[56:64].astype(BF16)
    text_ref[...] = rows[0:56].astype(BF16)


def on_device(vit, ln_gain, w_fc1, b_fc1, w_fc2, b_fc2, w_proj, b_proj, text, rms_gain, w_gate, w_up, w_out):
    vmem = pl.BlockSpec(memory_space=pltpu.VMEM)
    hbm = pl.BlockSpec(memory_space=pl.ANY)
    bf = lambda *shape: pltpu.VMEM(shape, BF16)
    f32 = lambda *shape: pltpu.VMEM(shape, F32)
    dma = pltpu.SemaphoreType.DMA
    vit_rows, result = pl.pallas_call(
        kernel,
        out_shape=(jax.ShapeDtypeStruct((64, 768), BF16), jax.ShapeDtypeStruct((64, DU), BF16)),
        in_specs=[hbm, vmem, hbm, vmem, hbm, vmem, hbm, vmem, hbm, vmem, hbm, hbm, hbm],
        out_specs=(vmem, vmem),
        scratch_shapes=[
            bf(64, 768), bf(56, DU), bf(768, 768), bf(768, 768),
            bf(4096, 1024), bf(4096, 1024), bf(16 * 1024, 256), bf(4 * 768, 256),
            f32(8, 8, 128), bf(16, 64, 768), bf(8, 8, 16, 768), bf(8, 8, 16, 768), bf(8, 8, 16, 768),
            bf(4, 8, 16, 768), bf(8, 4, 16, 768), bf(4, 64, 768),
            bf(8, 4, 16, 512), bf(8, 4, 16, 512), f32(4, 16, 512), f32(4, 16, 512),
            bf(8, EARLY, DU), bf(8, LATE, DU), f32(8 * EARLY, 1024), bf(8 * EARLY, 1024), bf(8 * LATE, 1024),
            bf(2, 4, EARLY, DU), bf(3, 2, EARLY, DU), bf(4, EARLY, DU), bf(EARLY, DU), bf(EARLY, DU),
            bf(8, LATE, DU), bf(8, LATE, DU), f32(LATE, DU),
            dma((3, 24)), dma((3, 20)), dma((12,)), dma((12,)), dma((8,)), dma((136,)), dma((156,)),
        ],
        compiler_params=pltpu.CompilerParams(
            collective_id=0, has_side_effects=True, vmem_limit_bytes=63 * 2**20
        ),
        cost_estimate=pl.CostEstimate(flops=15_300_000_000, bytes_accessed=12_000_000, transcendentals=1_000_000),
    )(vit, ln_gain, w_fc1, b_fc1, w_fc2, b_fc2, w_proj, b_proj, text, rms_gain, w_gate, w_up, w_out)
    return pl.pallas_call(
        split,
        out_shape=(
            jax.ShapeDtypeStruct((64, 768), BF16),
            jax.ShapeDtypeStruct((8, DU), BF16),
            jax.ShapeDtypeStruct((56, DU), BF16),
        ),
        in_specs=[vmem] * 2,
        out_specs=(vmem, vmem, vmem),
    )(vit_rows, result)


def solution(mesh):
    return jax.shard_map(
        on_device,
        mesh=mesh,
        in_specs=(
            P("wide", "narrow"),
            P("narrow"),
            P("narrow", "wide"),
            P("wide"),
            P("wide", "narrow"),
            P("narrow"),
            P("narrow", "wide"),
            P(),
            P(("wide", "narrow"), None),
            P(),
            P("wide", "narrow"),
            P("wide", "narrow"),
            P("narrow", "wide"),
        ),
        out_specs=(P("wide", "narrow"), P(("wide", "narrow"), None), P(("wide", "narrow"), None)),
        check_vma=False,
    )
```
